256 devices in a mesh: cand: 8 (over z_hi, x), hist: 32 (over z_lo, y, core).
Axes of the slice: x: 4, y: 4, z: 8 (z_hi: 2, z_lo: 4; z = z_hi * 4 + z_lo), core: 2. Of those that a mesh axis runs over, the one named last changes fastest.
Arguments:
- candidates: bfloat16 [2048, 512], P('cand'), may hold values from -6 to 6
- norm_gain: float32 [512], replicated, may hold values from 0.1 to 1.9
- qu_weight: bfloat16 [512, 1024], replicated, may hold values from -0.25 to 0.25
- out_weight: bfloat16 [512, 512], replicated, may hold values from -0.25 to 0.25
- kv_cache: bfloat16 [8192, 128, 1024], P(('cand', 'hist')), may hold values from -6 to 6
- requests: int32 [256, 16], P(('cand', 'hist')), may hold values from 0 to 8191, as said below
- block_mask: int32 [16, 8192], replicated, may hold values 0 or 1
- hist_len: int32 [8192], replicated, may hold values from 1 to 128
Outputs:
- scored: bfloat16 [2048, 512], P(('cand', 'hist'))
The draws below stay inside these ranges and needn't reach their ends.
Inputs may be any that keep to these rules, and one draw needn't show every extreme that they name: Each row holds 16 distinct block numbers; block b is held by device b // 32 in cand+hist order, and a device requests only blocks held by devices with its own cand index; no block is requested twice; a row holds at most 1 block of any one holder, and every holder is asked for exactly 16 distinct blocks, one by each of 16 devices of its cand group.
All inputs are finite; a program needn't handle non-finite values.
Results may differ from the reference program's by a relative error of at most 0.008.
Values may be sent and summed in bfloat16 or wider, within the bound.
No kernel may reach another device: no remote copies, remote signals or barrier semaphores. Data moves between devices by JAX's collectives and lax.ppermute only.
A program may use at most 128 MiB of HBM per device.

```python
import jax
import jax.numpy as jnp
from jax import lax

D = 512
H = 8
DH = 64
BLK = 128
REQ = 16
OWN = 32
NB = 8192
CANDS = 2048
CBLK = 16
N_CAND = 8
N_HIST = 32


def draw_requests(key, part):
    key = jax.random.fold_in(key, 7)
    subkeys = jax.random.split(key, 3)
    group_keys = jax.random.split(subkeys[0], N_CAND)
    orders = jax.vmap(lambda subkey: jax.random.permutation(subkey, N_HIST))(group_keys)
    slot_keys = jax.random.split(subkeys[1], N_CAND * N_HIST)
    slot_tables = jax.vmap(lambda subkey: jax.random.permutation(subkey, OWN))(slot_keys).reshape(N_CAND, N_HIST, OWN)
    requester = jnp.arange(N_HIST)[:, None]
    column = jnp.arange(REQ)[None, :]

    def one_group(group_index, order, slot_table):
        holder = (requester + order[column]) % N_HIST
        standing = jnp.broadcast_to(column, (N_HIST, REQ))
        picked = slot_table[holder, standing]
        return (group_index * N_HIST + holder) * OWN + picked
    numbers = jax.vmap(one_group)(jnp.arange(N_CAND), orders, slot_tables).reshape(N_CAND * N_HIST, REQ)
    row_keys = jax.random.split(subkeys[2], N_CAND * N_HIST)
    shuffles = jax.vmap(lambda subkey: jax.random.permutation(subkey, REQ))(row_keys)
    return jnp.take_along_axis(numbers, shuffles, axis=1).astype(jnp.int32)


def draw_hist_len(key, part):
    key = jax.random.fold_in(key, 5)
    subkeys = jax.random.split(key, 2)
    partial_rows = jax.random.randint(subkeys[0], (NB,), 1, BLK + 1)
    complete = jax.random.randint(subkeys[1], (NB,), 0, 4) > 0
    lengths = jnp.where(complete, BLK, partial_rows)
    lengths = lengths.at[0].set(BLK).at[1].set(1)
    return lengths.astype(jnp.int32)


def with_ends(drawn, key, least, top_value):
    place = [jax.random.randint(jax.random.fold_in(key, axis), (), 0, length) for axis, length in enumerate(drawn.shape)]
    longest = drawn.shape.index(max(drawn.shape))
    next_to = place[:longest] + [(place[longest] + 1) % drawn.shape[longest]] + place[longest + 1:]
    return drawn.at[tuple(place)].set(least).at[tuple(next_to)].set(top_value)


def levels(stream_key, dims, shards, least, largest):
    def one(dim, blocks):
        steps = jax.random.uniform(jax.random.fold_in(jax.random.fold_in(stream_key, 6), dim), (blocks,), jnp.float32, least / len(shards), largest / len(shards))
        return jnp.repeat(jnp.exp(steps), dims[dim] // blocks).reshape((-1,) + (1,) * (len(dims) - dim - 1))

    gain = one(*shards[0])
    for cut in shards[1:]:
        gain = gain * one(*cut)
    return gain


def noise(own_key, shape, scale, reach, cuts=(), kind=jnp.bfloat16):
    level = levels(own_key, shape, cuts, -0.22, 0.18) if cuts else 1.0
    drawn = jax.random.normal(own_key, shape, jnp.float32) * scale * level
    return jnp.minimum(jnp.maximum(drawn, -reach), reach).astype(kind)


def setup_inputs(seed: int = 0) -> dict:
    key_list = jax.random.split(jax.random.key(seed), 9)
    candidates = noise(key_list[0], (CANDS, D), 1.0, 6.0, ((0, 8),))
    norm_gain = jnp.clip(1.0 + 0.18 * jax.random.normal(key_list[1], (D,), jnp.float32), 0.1, 1.9)
    qu_weight = noise(key_list[2], (D, 2 * D), D ** -0.5, 0.25)
    out_weight = noise(key_list[3], (D, D), D ** -0.5, 0.25)
    kv_cache = noise(key_list[4], (NB, BLK, 2 * D), 1.0, 6.0, ((0, 256),))
    requests = draw_requests(jax.random.fold_in(key_list[8], 71), 0)
    block_mask = with_ends((jax.random.randint(key_list[6], (CBLK, NB), 0, 4) < 1).astype(jnp.int32), jax.random.fold_in(key_list[6], 1), 0, 1)
    hist_len = draw_hist_len(jax.random.fold_in(key_list[8], 71), 0)
    return dict(candidates=candidates, norm_gain=norm_gain, qu_weight=qu_weight, out_weight=out_weight, kv_cache=kv_cache, requests=requests, block_mask=block_mask, hist_len=hist_len)


EPS = 1e-05
SCALE = 0.125

def normalize_input(candidates, norm_gain):
    values = candidates.astype(jnp.float32)
    center = lax.optimization_barrier(jnp.mean(values, axis=-1, keepdims=True))
    spread = lax.optimization_barrier(jnp.mean(jnp.square(values - center), axis=-1, keepdims=True))
    return ((values - center) * lax.rsqrt(spread + EPS) * norm_gain).astype(jnp.bfloat16)

def head_norm(summed, gate_part):
    count = summed.shape[0]
    grouped = summed.reshape(count, H, DH)
    center = lax.optimization_barrier(jnp.mean(grouped, axis=-1, keepdims=True))
    spread = lax.optimization_barrier(jnp.mean(jnp.square(grouped - center), axis=-1, keepdims=True))
    normed = ((grouped - center) * lax.rsqrt(spread + EPS)).reshape(count, H * DH)
    return (normed * gate_part).astype(jnp.bfloat16)

def reference(candidates, norm_gain, qu_weight, out_weight, kv_cache, requests, block_mask, hist_len):
    normed_input = normalize_input(candidates, norm_gain)
    projected = jax.nn.silu(jnp.dot(normed_input, qu_weight, preferred_element_type=jnp.float32))
    queries = projected[:, :D].astype(jnp.bfloat16)
    gate_part = projected[:, D:]
    query_heads = queries.astype(jnp.float32).reshape(CANDS, H, DH)
    row_number = jnp.arange(BLK)[None, :]

    def visit(total, block_list):
        fetched = kv_cache[block_list].astype(jnp.float32)
        key_heads = fetched[:, :, :D].reshape(REQ * BLK, H, DH)
        value_heads = fetched[:, :, D:].reshape(REQ * BLK, H, DH)
        key_valid = (row_number < hist_len[block_list][:, None]).astype(jnp.float32).reshape(REQ * BLK)
        pair_mask = block_mask[:, block_list].astype(jnp.float32)
        weight_mask = jnp.repeat(jnp.repeat(pair_mask, BLK, axis=0), BLK, axis=1) * key_valid[None, :]
        scores = jnp.einsum('qhd,khd->hqk', query_heads, key_heads)
        weights = (jax.nn.silu(scores * SCALE) * weight_mask[None]).astype(jnp.bfloat16)
        weights = lax.optimization_barrier(weights).astype(jnp.float32)
        return (total + jnp.einsum('hqk,khd->qhd', weights, value_heads), None)
    summed, _ = lax.scan(visit, jnp.zeros((CANDS, H, DH), jnp.float32), requests)
    mixed = head_norm(summed.reshape(CANDS, D), gate_part)
    output = candidates.astype(jnp.float32) + jnp.dot(mixed, out_weight, preferred_element_type=jnp.float32)
    return output.astype(jnp.bfloat16)
```

```python
import jax
import jax.numpy as jnp
from jax import lax
from jax.experimental import pallas as pl
from jax.experimental.pallas import tpu as pltpu
from jax.sharding import Mesh, PartitionSpec as P

H = 8
DH = 64
D = H * DH
BLK = 128
OWN = 32
EPS = 1e-05
HALF_SCALE = 0.0625
LAST_DIMS = (((1,), (1,)), ((), ()))
AXES = ("zh", "x", "zl", "y", "c")
CAND = ("zh", "x")
HIST = ("zl", "y", "c")


def normalize_input(values, norm_gain):
    center = jnp.mean(values, axis=-1, keepdims=True)
    spread = jnp.mean(jnp.square(values - center), axis=-1, keepdims=True)
    return ((values - center) * lax.rsqrt(spread + EPS) * norm_gain).astype(jnp.bfloat16)


def head_norm(summed, gate_part):
    count = summed.shape[0]
    grouped = summed.reshape(count, H, DH)
    center = jnp.mean(grouped, axis=-1, keepdims=True)
    spread = jnp.mean(jnp.square(grouped - center), axis=-1, keepdims=True)
    normed = ((grouped - center) * lax.rsqrt(spread + EPS)).reshape(count, H * DH)
    return (normed * gate_part).astype(jnp.bfloat16)


def shift(value, axis, steps):
    count = lax.axis_size(axis)
    return lax.ppermute(value, axis, [(i, (i + steps) % count) for i in range(count)])


def attend_kernel(lists, counts, lens, used, me, own_ref, oth_ref, kv_ref, out_own, out_oth, kvs, qbd, acc, sem):
    def start(s, _):
        @pl.when(used[s] > 0)
        def _():
            pltpu.make_async_copy(kv_ref.at[s], kvs.at[s], sem.at[s]).start()

        return 0

    lax.fori_loop(0, OWN, start, 0)
    kvs[OWN] = jnp.zeros((BLK, 2 * D), jnp.bfloat16)

    def finish(s, _):
        @pl.when(used[s] > 0)
        def _():
            pltpu.make_async_copy(kv_ref.at[s], kvs.at[s], sem.at[s]).wait()

            @pl.when(lens[s] < BLK)
            def _():
                row = lax.broadcasted_iota(jnp.int32, (BLK, D), 0)
                values = kvs[s, :, D:].astype(jnp.float32)
                kvs[s, :, D:] = jnp.where(row < lens[s], values, 0.0).astype(jnp.bfloat16)

        return 0

    lax.fori_loop(0, OWN, finish, 0)
    head = lax.broadcasted_iota(jnp.int32, (BLK, 256), 1) // DH

    def block(i, _):
        cand = i // 2
        part = i % 2
        slot = lax.rem(me[0] - cand + 8, 8)
        first = pl.multiple_of(part * 64, 64)
        for g in range(2):
            cols = slice(g * 256, (g + 1) * 256)
            queries = jnp.concatenate([own_ref[slot, pl.ds(first, 64), cols], oth_ref[slot, pl.ds(first, 64), cols]], axis=0)
            for h in range(4):
                qbd[g, h * BLK : (h + 1) * BLK, :] = jnp.where(head == h, queries, jnp.zeros_like(queries))
        acc[...] = jnp.zeros_like(acc)

        def pair(p, _):
            a = lists[i, 2 * p]
            b = lists[i, 2 * p + 1]
            for g in range(2):
                kcols = slice(g * 256, (g + 1) * 256)
                vcols = slice(D + g * 256, D + (g + 1) * 256)
                keys = jnp.concatenate([kvs[a, :, kcols], kvs[b, :, kcols]], axis=0)
                values = jnp.concatenate([kvs[a, :, vcols], kvs[b, :, vcols]], axis=0)
                half = lax.dot_general(qbd[g], keys, LAST_DIMS, preferred_element_type=jnp.float32)
                weights = (half + half * jnp.tanh(half)).astype(jnp.bfloat16)
                acc[g] += jnp.dot(weights, values, preferred_element_type=jnp.float32)
            return 0

        lax.fori_loop(0, (counts[i] + 1) // 2, pair, 0)
        x = cand % 4
        z = cand // 4 * 2 + part
        for g in range(2):
            cols = slice(g * 256, (g + 1) * 256)
            total = acc[g, :BLK]
            for h in range(1, 4):
                total = jnp.where(head == h, acc[g, h * BLK : (h + 1) * BLK], total)
            total = total.astype(jnp.bfloat16)
            for y in range(4):
                out_own[x * 4 + y, z, :, cols] = total[y * 16 : (y + 1) * 16]
                out_oth[x * 4 + y, z, :, cols] = total[64 + y * 16 : 64 + (y + 1) * 16]
        return 0

    lax.fori_loop(0, 16, block, 0)


def attend(lists, counts, lens, used, me, own, oth, kv_cache):
    half = jax.ShapeDtypeStruct((16, 4, 16, D), jnp.bfloat16)
    vmem = pl.BlockSpec(memory_space=pltpu.VMEM)
    return pl.pallas_call(
        attend_kernel,
        grid_spec=pltpu.PrefetchScalarGridSpec(
            num_scalar_prefetch=5,
            grid=(),
            in_specs=[vmem, vmem, pl.BlockSpec(memory_space=pl.ANY)],
            out_specs=[vmem, vmem],
            scratch_shapes=[
                pltpu.VMEM((OWN + 1, BLK, 2 * D), jnp.bfloat16),
                pltpu.VMEM((2, 4 * BLK, 256), jnp.bfloat16),
                pltpu.VMEM((2, 4 * BLK, 256), jnp.float32),
                pltpu.SemaphoreType.DMA((OWN,)),
            ],
        ),
        out_shape=[half, half],
        compiler_params=pltpu.CompilerParams(vmem_limit_bytes=40 * 1024 * 1024),
        cost_estimate=pl.CostEstimate(flops=20_000_000_000, bytes_accessed=8_000_000, transcendentals=0),
        name="attend",
    )(lists, counts, lens, used, me, own, oth, kv_cache)


def on_device(candidates, norm_gain, qu_weight, out_weight, kv_cache, requests, block_mask, hist_len):
    zl, y, c = (lax.axis_index(a) for a in HIST)
    cand_index = lax.axis_index("zh") * 4 + lax.axis_index("x")
    hist_index = (zl * 4 + y) * 2 + c
    first_block = (cand_index * 32 + hist_index) * OWN

    wanted = requests[0]
    holder = wanted // OWN % 32
    to_holder = jnp.sum(
        jnp.where(holder[None, :] == jnp.arange(32)[:, None], wanted[None, :] % OWN + 1, 0), axis=1, keepdims=True
    )
    asked = lax.all_to_all(to_holder, HIST, 0, 0, tiled=True)

    grid = candidates.reshape(2, 2, 4, 2, 8, D)
    mine = lax.dynamic_index_in_dim(grid, c, 3, keepdims=False)
    mine = mine.transpose(0, 2, 1, 3, 4).reshape(128, D).astype(jnp.float32)
    projected = jnp.dot(normalize_input(mine, norm_gain), qu_weight[:, :D], preferred_element_type=jnp.float32)
    queries = jax.nn.silu(projected).astype(jnp.bfloat16) * jnp.bfloat16(HALF_SCALE)
    own = jnp.stack([queries] + [shift(queries, CAND, s) for s in range(1, 8)])
    oth = shift(own, "c", 1)

    slots = jnp.arange(OWN)
    used = jnp.sum((asked == slots[None, :] + 1).astype(jnp.int32), axis=0)
    mask = lax.dynamic_slice_in_dim(block_mask, first_block, OWN, 1)
    lens = lax.dynamic_slice_in_dim(hist_len, first_block, OWN, 0)
    active = (mask * used[None, :]) > 0
    before = slots[None, None, :] < slots[None, :, None]
    place = jnp.sum((active[:, None, :] & before).astype(jnp.int32), axis=2)
    counts = jnp.sum(active.astype(jnp.int32), axis=1)
    entry = jnp.arange(OWN + 2)
    chosen = active[:, None, :] & (place[:, None, :] == entry[None, :, None])
    lists = jnp.sum(jnp.where(chosen, slots[None, None, :], 0), axis=2)
    lists = jnp.where(entry[None, :] < counts[:, None], lists, OWN)

    to_own, to_oth = attend(lists, counts, lens, used, cand_index.reshape(1), own, oth, kv_cache)

    from_oth = shift(to_oth, "c", 1)
    summed = (to_own.astype(jnp.float32) + from_oth.astype(jnp.float32)).astype(jnp.bfloat16)
    parts = lax.all_to_all(summed.reshape(16, 64, D), ("x", "y"), 0, 0, tiled=True)
    summed = jnp.sum(parts.astype(jnp.float32), axis=0).astype(jnp.bfloat16)
    parts = lax.all_to_all(summed.reshape(8, 8, D), ("zh", "zl"), 0, 0, tiled=True)
    summed = jnp.sum(parts.astype(jnp.float32), axis=0)

    rows = lax.dynamic_slice_in_dim(candidates, hist_index * 8, 8, 0).astype(jnp.float32)
    gate = jax.nn.silu(
        jnp.dot(normalize_input(rows, norm_gain), qu_weight[:, D:], preferred_element_type=jnp.float32)
    )
    mixed = head_norm(summed, gate)
    output = rows + jnp.dot(mixed, out_weight, preferred_element_type=jnp.float32)
    return output.astype(jnp.bfloat16)


def solution(mesh):
    fine = Mesh(mesh.devices.reshape(2, 4, 4, 4, 2), AXES)
    placed = (
        P(CAND, None),
        P(),
        P(),
        P(),
        P(AXES, None, None),
        P(AXES, None),
        P(),
        P(),
    )
    return jax.shard_map(on_device, mesh=fine, in_specs=placed, out_specs=P(AXES, None), check_vma=False)
```

```python
import jax
import jax.numpy as jnp
from jax import lax
from jax.experimental import pallas as pl
from jax.experimental.pallas import tpu as pltpu
from jax.sharding import Mesh, PartitionSpec as P

H = 8
DH = 64
D = H * DH
BLK = 128
OWN = 32
EPS = 1e-05
HALF_SCALE = 0.0625
LAST_DIMS = (((1,), (1,)), ((), ()))
AXES = ("zh", "x", "zl", "y", "c")
CAND = ("zh", "x")
HIST = ("zl", "y", "c")
SLOTS = 2 * OWN
AT_ONCE = 3
ITEMS = 4 * OWN + 4 * AT_ONCE


def normalize_input(values, norm_gain):
    center = jnp.mean(values, axis=-1, keepdims=True)
    spread = jnp.mean(jnp.square(values - center), axis=-1, keepdims=True)
    return ((values - center) * lax.rsqrt(spread + EPS) * norm_gain).astype(jnp.bfloat16)


def silu(values):
    half = 0.5 * values
    return half + half * jnp.tanh(half)


def shift(value, axis, steps):
    count = lax.axis_size(axis)
    return lax.ppermute(value, axis, [(i, (i + steps) % count) for i in range(count)])


def project_kernel(place, cand_ref, gain_ref, weight_ref, query_ref, gate_ref):
    gain = gain_ref[...]
    mine = cand_ref[pl.ds(pl.multiple_of(place[0] * BLK, BLK), BLK), :].astype(jnp.float32)
    projected = jnp.dot(normalize_input(mine, gain), weight_ref[:, :D], preferred_element_type=jnp.float32)
    query_ref[...] = silu(projected).astype(jnp.bfloat16) * jnp.bfloat16(HALF_SCALE)
    rows = cand_ref[pl.ds(pl.multiple_of(place[1] * 16, 16), 16), :].astype(jnp.float32)
    gate_ref[...] = silu(jnp.dot(normalize_input(rows, gain), weight_ref[:, D:], preferred_element_type=jnp.float32))


def project(place, candidates, norm_gain, qu_weight):
    vmem = pl.BlockSpec(memory_space=pltpu.VMEM)
    return pl.pallas_call(
        project_kernel,
        grid_spec=pltpu.PrefetchScalarGridSpec(
            num_scalar_prefetch=1, grid=(), in_specs=[vmem, vmem, vmem], out_specs=[vmem, vmem]
        ),
        out_shape=[jax.ShapeDtypeStruct((BLK, D), jnp.bfloat16), jax.ShapeDtypeStruct((16, D), jnp.float32)],
        compiler_params=pltpu.CompilerParams(vmem_limit_bytes=16 * 1024 * 1024),
        name="project",
    )(place, candidates, norm_gain.reshape(1, D), qu_weight)


def finish_kernel(place, parts_ref, gate_ref, cand_ref, weight_ref, out_ref):
    summed = jnp.sum(parts_ref[...].astype(jnp.float32), axis=0)
    core = place[2]
    gate = jnp.where(core == 0, gate_ref[:8], gate_ref[8:])
    rows = cand_ref[pl.ds(pl.multiple_of(place[1] * 16, 16), 16), :].astype(jnp.float32)
    rows = jnp.where(core == 0, rows[:8], rows[8:])
    heads = []
    for h in range(H):
        one = summed[:, h * DH : (h + 1) * DH]
        center = jnp.mean(one, axis=-1, keepdims=True)
        spread = jnp.mean(jnp.square(one - center), axis=-1, keepdims=True)
        heads.append((one - center) * lax.rsqrt(spread + EPS))
    mixed = (jnp.concatenate(heads, axis=1) * gate).astype(jnp.bfloat16)
    output = rows + jnp.dot(mixed, weight_ref[...], preferred_element_type=jnp.float32)
    out_ref[...] = output.astype(jnp.bfloat16)


def finish(place, parts, gate, candidates, out_weight):
    vmem = pl.BlockSpec(memory_space=pltpu.VMEM)
    return pl.pallas_call(
        finish_kernel,
        grid_spec=pltpu.PrefetchScalarGridSpec(
            num_scalar_prefetch=1, grid=(), in_specs=[vmem] * 4, out_specs=vmem
        ),
        out_shape=jax.ShapeDtypeStruct((8, D), jnp.bfloat16),
        compiler_params=pltpu.CompilerParams(vmem_limit_bytes=16 * 1024 * 1024),
        name="finish",
    )(place, parts, gate, candidates, out_weight)


def attend_kernel(
    lists, item_block, item_pair, total, lens, used, place, *rest
):
    *q_refs, own_ref, oth_ref, out_ref, kvs, q_all, acc, held, sem = rest

    def start(s, _):
        @pl.when(used[s] > 0)
        def _():
            pltpu.make_async_copy(own_ref.at[s], kvs.at[s], sem.at[s]).start()

        @pl.when(used[OWN + s] > 0)
        def _():
            pltpu.make_async_copy(oth_ref.at[s], kvs.at[OWN + s], sem.at[OWN + s]).start()

        return 0

    lax.fori_loop(0, OWN, start, 0)
    kvs[SLOTS] = jnp.zeros((BLK, 2 * D), jnp.bfloat16)
    acc[...] = jnp.zeros_like(acc)
    for k, ref in enumerate(q_refs):
        q_all[k] = ref[...]

    def arrive(s, _):
        @pl.when(used[s] > 0)
        def _():
            pltpu.make_async_copy(own_ref.at[0], kvs.at[s], sem.at[s]).wait()

            @pl.when(lens[s] < BLK)
            def _():
                row = lax.broadcasted_iota(jnp.int32, (BLK, D), 0)
                values = kvs[s, :, D:].astype(jnp.float32)
                kvs[s, :, D:] = jnp.where(row < lens[s], values, 0.0).astype(jnp.bfloat16)

        return 0

    lax.fori_loop(0, SLOTS, arrive, 0)
    head = lax.broadcasted_iota(jnp.int32, (BLK, 256), 1) // DH
    my_zh = place[3]
    my_x = place[4]

    def weights(t, g):
        i = item_block[t]
        p = item_pair[t]
        a = lists[i, 2 * p]
        b = lists[i, 2 * p + 1]
        slot = jnp.where(i // 4 == my_zh, 0, 4) + lax.rem(my_x - i % 4 + 4, 4)
        cols = slice(g * 256, (g + 1) * 256)
        keys = jnp.concatenate([kvs[a, :, cols], kvs[b, :, cols]], axis=0)
        queries = q_all[slot, :, cols]
        spread = jnp.concatenate([jnp.where(head == h, queries, jnp.zeros_like(queries)) for h in range(4)], axis=0)
        half = lax.dot_general(spread, keys, LAST_DIMS, preferred_element_type=jnp.float32)
        return (half + half * jnp.tanh(half)).astype(jnp.bfloat16)

    def attended(t, g, weight):
        i = item_block[t]
        p = item_pair[t]
        a = lists[i, 2 * p]
        b = lists[i, 2 * p + 1]
        cols = slice(D + g * 256, D + (g + 1) * 256)
        values = jnp.concatenate([kvs[a, :, cols], kvs[b, :, cols]], axis=0)
        every = jnp.dot(weight, values, preferred_element_type=jnp.float32)
        mine = every[:BLK]
        for h in range(1, 4):
            mine = jnp.where(head == h, every[h * BLK : (h + 1) * BLK], mine)
        return mine

    def fill(n, slot):
        for u in range(AT_ONCE):
            for g in range(2):
                held[slot, u, g] = weights(n * AT_ONCE + u, g)

    fill(0, 0)

    def step(n, _):
        now = n % 2
        sums = [attended(n * AT_ONCE + u, g, held[now, u, g]) for u in range(AT_ONCE) for g in range(2)]
        fill(n + 1, 1 - now)
        for u in range(AT_ONCE):
            i = item_block[n * AT_ONCE + u]
            for g in range(2):
                acc[i, :, g * 256 : (g + 1) * 256] += sums[2 * u + g]
        return 0

    lax.fori_loop(0, (total[0] + AT_ONCE - 1) // AT_ONCE, step, 0)
    for i in range(8):
        for z in range(2):
            for y in range(4):
                first = z * 64 + y * 16
                out_ref[i % 4 * 4 + y, i // 4 * 2 + z] = acc[i, first : first + 16, :].astype(jnp.bfloat16)


def attend(scalars, queries, own, oth):
    vmem = pl.BlockSpec(memory_space=pltpu.VMEM)
    hbm = pl.BlockSpec(memory_space=pltpu.HBM)
    return pl.pallas_call(
        attend_kernel,
        grid_spec=pltpu.PrefetchScalarGridSpec(
            num_scalar_prefetch=len(scalars),
            grid=(),
            in_specs=[vmem] * 8 + [hbm, hbm],
            out_specs=vmem,
            scratch_shapes=[
                pltpu.VMEM((SLOTS + 1, BLK, 2 * D), jnp.bfloat16),
                pltpu.VMEM((8, BLK, D), jnp.bfloat16),
                pltpu.VMEM((8, BLK, D), jnp.float32),
                pltpu.VMEM((2, AT_ONCE, 2, 4 * BLK, 256), jnp.bfloat16),
                pltpu.SemaphoreType.DMA((SLOTS,)),
            ],
        ),
        out_shape=jax.ShapeDtypeStruct((16, 4, 16, D), jnp.bfloat16),
        compiler_params=pltpu.CompilerParams(vmem_limit_bytes=50 * 1024 * 1024),
        cost_estimate=pl.CostEstimate(flops=20_000_000_000, bytes_accessed=8_000_000, transcendentals=0),
        name="attend",
    )(*scalars, *queries, own, oth)


def on_device(candidates, norm_gain, qu_weight, out_weight, kv_cache, requests, block_mask, hist_len):
    zh, x, zl, y, c = (lax.axis_index(a) for a in AXES)
    hist_index = (zl * 4 + y) * 2 + c
    first_block = ((zh * 4 + x) * 32 + zl * 8 + y * 2) * OWN
    place = jnp.stack([c, zl * 4 + y, c, zh, x]).astype(jnp.int32)

    oth_cache = shift(kv_cache, "c", 1)

    wanted = requests[0]
    holder = wanted // OWN % 32
    to_holder = jnp.sum(
        jnp.where(holder[None, :] == jnp.arange(32)[:, None], wanted[None, :] % OWN + 1, 0), axis=1
    ).reshape(16, 2)
    to_holder = jnp.stack([to_holder, to_holder[:, ::-1]], axis=-1).reshape(32, 2)
    asked = lax.all_to_all(to_holder, HIST, 0, 0, tiled=True)

    queries, gate = project(place, candidates, norm_gain, qu_weight)
    near = [queries] + [shift(queries, "x", s) for s in range(1, 4)]
    across = shift(queries, "zh", 1)
    across, asked = lax.optimization_barrier((across, asked))
    far = [across] + [shift(across, "x", s) for s in range(1, 4)]

    slots = jnp.arange(OWN)
    used = jnp.sum((asked[:, :, None] == slots[None, None, :] + 1).astype(jnp.int32), axis=0).reshape(SLOTS)
    mask = lax.dynamic_slice_in_dim(block_mask, first_block, SLOTS, 1).reshape(8, 2, 2, OWN)
    mask = lax.dynamic_index_in_dim(mask, c, 1, keepdims=False)
    mask = jnp.where(c == 0, mask, mask[:, ::-1]).reshape(8, SLOTS)
    lens = lax.dynamic_slice_in_dim(hist_len, first_block, SLOTS, 0).reshape(2, OWN)
    lens = jnp.where(c == 0, lens, lens[::-1]).reshape(SLOTS)
    active = (mask * used[None, :]) > 0
    slots = jnp.arange(SLOTS)
    before = slots[None, None, :] < slots[None, :, None]
    order = jnp.sum((active[:, None, :] & before).astype(jnp.int32), axis=2)
    counts = jnp.sum(active.astype(jnp.int32), axis=1)
    entry = jnp.arange(OWN + 4)
    chosen = active[:, None, :] & (order[:, None, :] == entry[None, :, None])
    lists = jnp.sum(jnp.where(chosen, slots[None, None, :], 0), axis=2)
    lists = jnp.where(entry[None, :] < counts[:, None], lists, SLOTS)
    pairs = (counts + 1) // 2
    blocks = jnp.arange(8)
    ends = jnp.sum(jnp.where(blocks[None, :] <= blocks[:, None], pairs[None, :], 0), axis=1)
    item = jnp.arange(ITEMS)
    past = item[:, None] >= ends[None, :]
    spare = item >= ends[7]
    item_block = jnp.where(spare, 7, jnp.sum(past.astype(jnp.int32), axis=1))
    item_pair = jnp.where(spare, OWN // 2, item - jnp.sum(jnp.where(past, pairs[None, :], 0), axis=1))
    scalars = (lists, item_block, item_pair, ends[7:], lens, used, place)

    sums = attend(scalars, near + far, kv_cache, oth_cache)

    parts = lax.all_to_all(sums.reshape(16, 64, D), ("x", "y"), 0, 0, tiled=True)
    sums = jnp.sum(parts.astype(jnp.float32), axis=0).astype(jnp.bfloat16).reshape(2, 1, 4, 8, D)
    sums = jnp.where(jnp.arange(2)[None, :, None, None, None] == c, sums, jnp.zeros_like(sums))
    parts = lax.all_to_all(sums.reshape(16, 8, D), ("zh", "zl", "c"), 0, 0, tiled=True)
    return finish(place, parts, gate, candidates, out_weight)


def solution(mesh):
    fine = Mesh(mesh.devices.reshape(2, 4, 4, 4, 2), AXES)
    placed = (
        P(CAND, None),
        P(),
        P(),
        P(),
        P(AXES, None, None),
        P(AXES, None),
        P(),
        P(),
    )
    return jax.shard_map(on_device, mesh=fine, in_specs=placed, out_specs=P(AXES, None), check_vma=False)
```

```python
import jax
import jax.numpy as jnp
from jax import lax
from jax.experimental import pallas as pl
from jax.experimental.pallas import tpu as pltpu
from jax.sharding import Mesh, PartitionSpec as P

H = 8
DH = 64
D = H * DH
BLK = 128
OWN = 32
EPS = 1e-05
HALF_SCALE = 0.0625
LAST_DIMS = (((1,), (1,)), ((), ()))
AXES = ("zh", "x", "zl", "y", "c")
CAND = ("zh", "x")
HIST = ("zl", "y", "c")
SLOTS = 2 * OWN
AT_ONCE = 3
ITEMS = 2 * OWN + 4 * AT_ONCE


def normalize_input(values, norm_gain):
    center = jnp.mean(values, axis=-1, keepdims=True)
    spread = jnp.mean(jnp.square(values - center), axis=-1, keepdims=True)
    return ((values - center) * lax.rsqrt(spread + EPS) * norm_gain).astype(jnp.bfloat16)


def silu(values):
    half = 0.5 * values
    return half + half * jnp.tanh(half)


def shift(value, axis, steps):
    count = lax.axis_size(axis)
    return lax.ppermute(value, axis, [(i, (i + steps) % count) for i in range(count)])


def project_kernel(place, cand_hbm, gain_hbm, weight_hbm, query_ref, cand, gain, weight, sem):
    first = pl.multiple_of(place[0] * BLK, BLK)
    copies = [
        pltpu.make_async_copy(weight_hbm.at[:, pl.ds(0, D)], weight, sem.at[0]),
        pltpu.make_async_copy(cand_hbm.at[pl.ds(first, BLK), :], cand, sem.at[1]),
        pltpu.make_async_copy(gain_hbm, gain, sem.at[2]),
    ]
    for copy in copies:
        copy.start()
    copies[1].wait()
    copies[2].wait()
    normed = normalize_input(cand[...].astype(jnp.float32), gain[...])
    copies[0].wait()
    projected = jnp.dot(normed, weight[...], preferred_element_type=jnp.float32)
    query_ref[...] = silu(projected).astype(jnp.bfloat16) * jnp.bfloat16(HALF_SCALE)


def project(place, candidates, norm_gain, qu_weight):
    hbm = pl.BlockSpec(memory_space=pltpu.HBM)
    return pl.pallas_call(
        project_kernel,
        grid_spec=pltpu.PrefetchScalarGridSpec(
            num_scalar_prefetch=1,
            grid=(),
            in_specs=[hbm, hbm, hbm],
            out_specs=pl.BlockSpec(memory_space=pltpu.VMEM),
            scratch_shapes=[
                pltpu.VMEM((BLK, D), jnp.bfloat16),
                pltpu.VMEM((1, D), jnp.float32),
                pltpu.VMEM((D, D), jnp.bfloat16),
                pltpu.SemaphoreType.DMA((3,)),
            ],
        ),
        out_shape=jax.ShapeDtypeStruct((BLK, D), jnp.bfloat16),
        compiler_params=pltpu.CompilerParams(vmem_limit_bytes=62 * 1024 * 1024),
        name="project",
    )(place, candidates, norm_gain.reshape(1, D), qu_weight)


def gate_kernel(place, cand_ref, gain_ref, weight_ref, gate_ref):
    rows = cand_ref[pl.ds(pl.multiple_of(place[1] * 16, 16), 16), :].astype(jnp.float32)
    normed = normalize_input(rows, gain_ref[...])
    gate_ref[...] = silu(jnp.dot(normed, weight_ref[:, D:], preferred_element_type=jnp.float32))


def project_gate(place, candidates, norm_gain, qu_weight):
    vmem = pl.BlockSpec(memory_space=pltpu.VMEM)
    return pl.pallas_call(
        gate_kernel,
        grid_spec=pltpu.PrefetchScalarGridSpec(
            num_scalar_prefetch=1, grid=(), in_specs=[vmem, vmem, vmem], out_specs=vmem
        ),
        out_shape=jax.ShapeDtypeStruct((16, D), jnp.float32),
        compiler_params=pltpu.CompilerParams(vmem_limit_bytes=16 * 1024 * 1024),
        name="gate",
    )(place, candidates, norm_gain.reshape(1, D), qu_weight)


def finish_kernel(place, parts_ref, gate_ref, cand_ref, weight_ref, out_ref):
    summed = jnp.sum(parts_ref[...].astype(jnp.float32), axis=0)
    core = place[2]
    gate = jnp.where(core == 0, gate_ref[:8], gate_ref[8:])
    rows = cand_ref[pl.ds(pl.multiple_of(place[1] * 16, 16), 16), :].astype(jnp.float32)
    rows = jnp.where(core == 0, rows[:8], rows[8:])
    heads = []
    for h in range(H):
        one = summed[:, h * DH : (h + 1) * DH]
        center = jnp.mean(one, axis=-1, keepdims=True)
        spread = jnp.mean(jnp.square(one - center), axis=-1, keepdims=True)
        heads.append((one - center) * lax.rsqrt(spread + EPS))
    mixed = (jnp.concatenate(heads, axis=1) * gate).astype(jnp.bfloat16)
    output = rows + jnp.dot(mixed, weight_ref[...], preferred_element_type=jnp.float32)
    out_ref[...] = output.astype(jnp.bfloat16)


def finish(place, parts, gate, candidates, out_weight):
    vmem = pl.BlockSpec(memory_space=pltpu.VMEM)
    return pl.pallas_call(
        finish_kernel,
        grid_spec=pltpu.PrefetchScalarGridSpec(
            num_scalar_prefetch=1, grid=(), in_specs=[vmem] * 4, out_specs=vmem
        ),
        out_shape=jax.ShapeDtypeStruct((8, D), jnp.bfloat16),
        compiler_params=pltpu.CompilerParams(vmem_limit_bytes=16 * 1024 * 1024),
        name="finish",
    )(place, parts, gate, candidates, out_weight)


def attend_kernel(lists, item_block, item_pair, total, source, lens, place, *rest):
    q0, q1, q2, q3, own_ref, oth_ref, out_ref, kvs, q_all, acc, held, sem = rest

    def start(k, _):
        s = source[k]

        @pl.when(s % 2 == 0)
        def _():
            pltpu.make_async_copy(own_ref.at[s // 2], kvs.at[k], sem.at[k]).start()

        @pl.when(s % 2 == 1)
        def _():
            pltpu.make_async_copy(oth_ref.at[s // 2], kvs.at[k], sem.at[k]).start()

        return 0

    lax.fori_loop(0, OWN, start, 0)
    kvs[OWN] = jnp.zeros((BLK, 2 * D), jnp.bfloat16)
    acc[...] = jnp.zeros_like(acc)
    for k, ref in enumerate((q0, q1, q2, q3)):
        q_all[k] = ref[...]

    def arrive(k, _):
        pltpu.make_async_copy(own_ref.at[0], kvs.at[k], sem.at[k]).wait()

        @pl.when(lens[k] < BLK)
        def _():
            row = lax.broadcasted_iota(jnp.int32, (BLK, D), 0)
            values = kvs[k, :, D:].astype(jnp.float32)
            kvs[k, :, D:] = jnp.where(row < lens[k], values, 0.0).astype(jnp.bfloat16)

        return 0

    def ensure(n, arrived):
        upto = arrived
        for u in range(AT_ONCE):
            i = item_block[n * AT_ONCE + u]
            p = item_pair[n * AT_ONCE + u]
            for part in range(2):
                block = lists[i, 2 * p + part]
                upto = jnp.maximum(upto, jnp.where(block < OWN, block + 1, 0))
        lax.fori_loop(arrived, upto, arrive, 0)
        return upto

    head = lax.broadcasted_iota(jnp.int32, (BLK, 256), 1) // DH
    my_x = place[4]

    def weights(t, g):
        i = item_block[t]
        p = item_pair[t]
        a = lists[i, 2 * p]
        b = lists[i, 2 * p + 1]
        slot = lax.rem(my_x - i + 4, 4)
        cols = slice(g * 256, (g + 1) * 256)
        keys = jnp.concatenate([kvs[a, :, cols], kvs[b, :, cols]], axis=0)
        queries = q_all[slot, :, cols]
        spread = jnp.concatenate([jnp.where(head == h, queries, jnp.zeros_like(queries)) for h in range(4)], axis=0)
        half = lax.dot_general(spread, keys, LAST_DIMS, preferred_element_type=jnp.float32)
        return (half + half * jnp.tanh(half)).astype(jnp.bfloat16)

    def attended(t, g, weight):
        i = item_block[t]
        p = item_pair[t]
        a = lists[i, 2 * p]
        b = lists[i, 2 * p + 1]
        cols = slice(D + g * 256, D + (g + 1) * 256)
        values = jnp.concatenate([kvs[a, :, cols], kvs[b, :, cols]], axis=0)
        every = jnp.dot(weight, values, preferred_element_type=jnp.float32)
        mine = every[:BLK]
        for h in range(1, 4):
            mine = jnp.where(head == h, every[h * BLK : (h + 1) * BLK], mine)
        return mine

    def fill(n, slot):
        for u in range(AT_ONCE):
            for g in range(2):
                held[slot, u, g] = weights(n * AT_ONCE + u, g)

    arrived = ensure(0, jnp.int32(0))
    fill(0, 0)

    def step(n, arrived):
        now = n % 2
        arrived = ensure(n + 1, arrived)
        sums = [attended(n * AT_ONCE + u, g, held[now, u, g]) for u in range(AT_ONCE) for g in range(2)]
        fill(n + 1, 1 - now)
        for u in range(AT_ONCE):
            i = item_block[n * AT_ONCE + u]
            for g in range(2):
                acc[i, :, g * 256 : (g + 1) * 256] += sums[2 * u + g]
        return arrived

    arrived = lax.fori_loop(0, (total[0] + AT_ONCE - 1) // AT_ONCE, step, arrived)
    lax.fori_loop(arrived, OWN, arrive, 0)
    for i in range(4):
        for z in range(2):
            for y in range(4):
                first = z * 64 + y * 16
                out_ref[i * 4 + y, z] = acc[i, first : first + 16, :].astype(jnp.bfloat16)


def attend(scalars, queries, own, oth):
    vmem = pl.BlockSpec(memory_space=pltpu.VMEM)
    hbm = pl.BlockSpec(memory_space=pltpu.HBM)
    return pl.pallas_call(
        attend_kernel,
        grid_spec=pltpu.PrefetchScalarGridSpec(
            num_scalar_prefetch=len(scalars),
            grid=(),
            in_specs=[vmem] * 4 + [hbm] * 2,
            out_specs=vmem,
            scratch_shapes=[
                pltpu.VMEM((OWN + 1, BLK, 2 * D), jnp.bfloat16),
                pltpu.VMEM((4, BLK, D), jnp.bfloat16),
                pltpu.VMEM((4, BLK, D), jnp.float32),
                pltpu.VMEM((2, AT_ONCE, 2, 4 * BLK, 256), jnp.bfloat16),
                pltpu.SemaphoreType.DMA((OWN,)),
            ],
        ),
        out_shape=jax.ShapeDtypeStruct((16, 2, 16, D), jnp.bfloat16),
        compiler_params=pltpu.CompilerParams(vmem_limit_bytes=52 * 1024 * 1024),
        cost_estimate=pl.CostEstimate(flops=10_000_000_000, bytes_accessed=8_000_000, transcendentals=0),
        name="attend",
    )(*scalars, *queries, own, oth)


def work_lists(active, position):
    slots = jnp.arange(SLOTS)
    before = slots[None, None, :] < slots[None, :, None]
    order = jnp.sum((active[:, None, :] & before).astype(jnp.int32), axis=2)
    counts = jnp.sum(active.astype(jnp.int32), axis=1)
    entry = jnp.arange(OWN + 4)
    chosen = active[:, None, :] & (order[:, None, :] == entry[None, :, None])
    lists = jnp.sum(jnp.where(chosen, position[None, None, :], 0), axis=2)
    lists = jnp.where(entry[None, :] < counts[:, None], lists, OWN)
    pairs = ((counts + 1) // 2).reshape(2, 4)
    pair = jnp.arange(OWN // 2)
    earlier = jnp.arange(4)[None, :] < jnp.arange(4)[:, None]
    level = jnp.sum(jnp.minimum(pairs[:, None, :], pair[None, :, None]), axis=2)
    same = jnp.sum((earlier[None, :, :, None] & (pairs[:, None, :, None] > pair)).astype(jnp.int32), axis=2)
    index = jnp.where(pairs[:, :, None] > pair, level[:, None, :] + same, -1).reshape(2, 1, 2 * OWN)
    here = jnp.arange(ITEMS)[None, :, None] == index
    code = jnp.arange(2 * OWN)
    spare = 3 * (OWN // 2) + OWN // 2
    found = jnp.sum(jnp.where(here, code - spare, 0), axis=2) + spare
    totals = jnp.sum(pairs, axis=1, keepdims=True)
    unused = found == spare
    item_block = jnp.where(unused, 3, found // (OWN // 2))
    item_pair = jnp.where(unused, OWN // 2, found % (OWN // 2))
    return lists, item_block, item_pair, totals


def on_device(candidates, norm_gain, qu_weight, out_weight, kv_cache, requests, block_mask, hist_len):
    zh, x, zl, y, c = (lax.axis_index(a) for a in AXES)
    first_block = ((zh * 4 + x) * 32 + zl * 8 + y * 2) * OWN
    place = jnp.stack([c, zl * 4 + y, c, zh, x]).astype(jnp.int32)

    oth_cache = shift(kv_cache, "c", 1)

    wanted = requests[0]
    holder = wanted // OWN % 32
    to_holder = jnp.sum(
        jnp.where(holder[None, :] == jnp.arange(32)[:, None], wanted[None, :] % OWN + 1, 0), axis=1
    ).reshape(16, 2)
    to_holder = jnp.stack([to_holder, to_holder[:, ::-1]], axis=-1).reshape(32, 2)
    asked = lax.all_to_all(to_holder, HIST, 0, 0, tiled=True)

    queries = project(place, candidates, norm_gain, qu_weight)
    across = shift(queries, "zh", 1)
    queries, asked = lax.optimization_barrier((queries, asked))
    near = [queries] + [shift(queries, "x", s) for s in range(1, 4)]
    far = [across] + [shift(across, "x", s) for s in range(1, 4)]

    slots = jnp.arange(OWN)
    used = jnp.sum((asked[:, None, :] == slots[None, :, None] + 1).astype(jnp.int32), axis=0).reshape(SLOTS)
    lens = lax.dynamic_slice_in_dim(hist_len, first_block, SLOTS, 0).reshape(2, OWN)
    lens = jnp.where(c == 0, lens, lens[::-1]).T.reshape(SLOTS)
    mask = lax.dynamic_slice_in_dim(block_mask, first_block, SLOTS, 1).reshape(2, 4, 2, 2, OWN)
    mask = lax.dynamic_index_in_dim(mask, c, 2, keepdims=False)
    mask = jnp.where(c == 0, mask, mask[:, :, ::-1])
    mask = jnp.where(zh == 0, mask, mask[::-1]).swapaxes(2, 3).reshape(8, SLOTS)
    slots = jnp.arange(SLOTS)
    position = jnp.sum(jnp.where(slots[None, :] < slots[:, None], used[None, :], 0), axis=1)
    at = (position[None, :] == jnp.arange(OWN)[:, None]) & (used[None, :] > 0)
    source = jnp.sum(jnp.where(at, slots[None, :], 0), axis=1)
    lens = jnp.sum(jnp.where(at, lens[None, :], 0), axis=1)
    lists, item_block, item_pair, totals = work_lists((mask * used[None, :]) > 0, position)

    summed = []
    for k, part in enumerate((near, far)):
        scalars = (lists[4 * k : 4 * k + 4], item_block[k], item_pair[k], totals[k], source, lens, place)
        sums = attend(scalars, part, kv_cache, oth_cache)
        parts = lax.all_to_all(sums.reshape(16, 32, D), ("x", "y"), 0, 0, tiled=True)
        summed.append(jnp.sum(parts.astype(jnp.float32), axis=0).astype(jnp.bfloat16).reshape(1, 1, 4, 8, D))

    own_zh = jnp.arange(2)[:, None, None, None, None] == zh
    own_parity = jnp.arange(2)[None, :, None, None, None] == c
    sums = jnp.where(own_parity, jnp.where(own_zh, summed[0], summed[1]), jnp.bfloat16(0))
    parts = lax.all_to_all(sums.reshape(16, 8, D), ("zh", "zl", "c"), 0, 0, tiled=True)
    gate = project_gate(place, candidates, norm_gain, qu_weight)
    return finish(place, parts, gate, candidates, out_weight)


def solution(mesh):
    fine = Mesh(mesh.devices.reshape(2, 4, 4, 4, 2), AXES)
    placed = (
        P(CAND, None),
        P(),
        P(),
        P(),
        P(AXES, None, None),
        P(AXES, None),
        P(),
        P(),
    )
    return jax.shard_map(on_device, mesh=fine, in_specs=placed, out_specs=P(AXES, None), check_vma=False)
```

```python
import functools

import jax
import jax.numpy as jnp
from jax import lax
from jax.experimental import pallas as pl
from jax.experimental.pallas import tpu as pltpu
from jax.sharding import Mesh, PartitionSpec as P

H = 8
DH = 64
D = H * DH
BLK = 128
OWN = 32
EPS = 1e-05
HALF_SCALE = 0.0625
LAST_DIMS = (((1,), (1,)), ((), ()))
AXES = ("zh", "x", "zl", "y", "c")
CAND = ("zh", "x")
HIST = ("zl", "y", "c")
SLOTS = 2 * OWN
AT_ONCE = 3
ITEMS = 4 * OWN + 4 * AT_ONCE
LIST = OWN + 4
BLOCK_AT = 8 * LIST
PAIR_AT = BLOCK_AT + ITEMS
SOURCE_AT = PAIR_AT + ITEMS
ROWS_AT = SOURCE_AT + OWN + 8
TOTAL_AT = ROWS_AT + OWN + 8
PLAN = TOTAL_AT + 8


def normalize_input(values, norm_gain):
    center = jnp.mean(values, axis=-1, keepdims=True)
    spread = jnp.mean(jnp.square(values - center), axis=-1, keepdims=True)
    return ((values - center) * lax.rsqrt(spread + EPS) * norm_gain).astype(jnp.bfloat16)


def silu(values):
    half = 0.5 * values
    return half + half * jnp.tanh(half)


def shift(value, axis, steps):
    count = lax.axis_size(axis)
    return lax.ppermute(value, axis, [(i, (i + steps) % count) for i in range(count)])


def project_kernel(near_rows, far_rows, gain, weight, near_ref, far_ref):
    rows = jnp.concatenate([near_rows[...], far_rows[...]], axis=0).astype(jnp.float32)
    projected = jnp.dot(normalize_input(rows, gain[...]), weight[:, :D], preferred_element_type=jnp.float32)
    queries = silu(projected).astype(jnp.bfloat16) * jnp.bfloat16(HALF_SCALE)
    near_ref[...] = queries[:BLK]
    far_ref[...] = queries[BLK:]


def project(near, far, norm_gain, qu_weight):
    vmem = pl.BlockSpec(memory_space=pltpu.VMEM)
    return pl.pallas_call(
        project_kernel,
        in_specs=[vmem] * 4,
        out_specs=[vmem] * 2,
        out_shape=[jax.ShapeDtypeStruct((BLK, D), jnp.bfloat16)] * 2,
        compiler_params=pltpu.CompilerParams(vmem_limit_bytes=16 * 1024 * 1024),
        name="project",
    )(near, far, norm_gain.reshape(1, D), qu_weight)


def gate_kernel(place, cand_ref, gain_ref, weight_ref, gate_ref):
    rows = cand_ref[pl.ds(pl.multiple_of(place[1] * 16, 16), 16), :].astype(jnp.float32)
    normed = normalize_input(rows, gain_ref[...])
    gate_ref[...] = silu(jnp.dot(normed, weight_ref[:, D:], preferred_element_type=jnp.float32))


def project_gate(place, candidates, norm_gain, qu_weight):
    vmem = pl.BlockSpec(memory_space=pltpu.VMEM)
    return pl.pallas_call(
        gate_kernel,
        grid_spec=pltpu.PrefetchScalarGridSpec(
            num_scalar_prefetch=1, grid=(), in_specs=[vmem, vmem, vmem], out_specs=vmem
        ),
        out_shape=jax.ShapeDtypeStruct((16, D), jnp.float32),
        compiler_params=pltpu.CompilerParams(vmem_limit_bytes=16 * 1024 * 1024),
        name="gate",
    )(place, candidates, norm_gain.reshape(1, D), qu_weight)


def finish_kernel(place, parts_ref, gate_ref, cand_ref, weight_ref, out_ref):
    summed = jnp.sum(parts_ref[...].astype(jnp.float32), axis=0)
    core = place[0]
    gate = jnp.where(core == 0, gate_ref[:8], gate_ref[8:])
    rows = cand_ref[pl.ds(pl.multiple_of(place[1] * 16, 16), 16), :].astype(jnp.float32)
    rows = jnp.where(core == 0, rows[:8], rows[8:])
    heads = []
    for h in range(H):
        one = summed[:, h * DH : (h + 1) * DH]
        center = jnp.mean(one, axis=-1, keepdims=True)
        spread = jnp.mean(jnp.square(one - center), axis=-1, keepdims=True)
        heads.append((one - center) * lax.rsqrt(spread + EPS))
    mixed = (jnp.concatenate(heads, axis=1) * gate).astype(jnp.bfloat16)
    output = rows + jnp.dot(mixed, weight_ref[...], preferred_element_type=jnp.float32)
    out_ref[...] = output.astype(jnp.bfloat16)


def finish(place, parts, gate, candidates, out_weight):
    vmem = pl.BlockSpec(memory_space=pltpu.VMEM)
    return pl.pallas_call(
        finish_kernel,
        grid_spec=pltpu.PrefetchScalarGridSpec(
            num_scalar_prefetch=1, grid=(), in_specs=[vmem] * 4, out_specs=vmem
        ),
        out_shape=jax.ShapeDtypeStruct((8, D), jnp.bfloat16),
        compiler_params=pltpu.CompilerParams(vmem_limit_bytes=16 * 1024 * 1024),
        name="finish",
    )(place, parts, gate, candidates, out_weight)


def attend_kernel(work, *rest):
    *q_refs, own_ref, oth_ref, out_ref, kvs, q_all, acc, held, sem = rest

    def start(k, _):
        s = work[SOURCE_AT + k]

        @pl.when(s % 2 == 0)
        def _():
            pltpu.make_async_copy(own_ref.at[s // 2], kvs.at[k], sem.at[k]).start()

        @pl.when(s % 2 == 1)
        def _():
            pltpu.make_async_copy(oth_ref.at[s // 2], kvs.at[k], sem.at[k]).start()

        return 0

    lax.fori_loop(0, OWN, start, 0)
    kvs[OWN] = jnp.zeros((BLK, 2 * D), jnp.bfloat16)
    acc[...] = jnp.zeros_like(acc)
    for k, ref in enumerate(q_refs):
        q_all[k] = ref[...]

    def arrive(k, _):
        pltpu.make_async_copy(own_ref.at[0], kvs.at[k], sem.at[k]).wait()

        @pl.when(work[ROWS_AT + k] < BLK)
        def _():
            row = lax.broadcasted_iota(jnp.int32, (BLK, D), 0)
            values = kvs[k, :, D:].astype(jnp.float32)
            kvs[k, :, D:] = jnp.where(row < work[ROWS_AT + k], values, 0.0).astype(jnp.bfloat16)

        return 0

    def ensure(n, arrived):
        upto = arrived
        for u in range(AT_ONCE):
            i = work[BLOCK_AT + n * AT_ONCE + u]
            p = work[PAIR_AT + n * AT_ONCE + u]
            for part in range(2):
                block = work[i * LIST + 2 * p + part]
                upto = jnp.maximum(upto, jnp.where(block < OWN, block + 1, 0))
        lax.fori_loop(arrived, upto, arrive, 0)
        return upto

    head = lax.broadcasted_iota(jnp.int32, (BLK, 256), 1) // DH
    my_x = work[TOTAL_AT + 1]

    def weights(t, g):
        i = work[BLOCK_AT + t]
        p = work[PAIR_AT + t]
        a = work[i * LIST + 2 * p]
        b = work[i * LIST + 2 * p + 1]
        slot = i // 4 * 4 + lax.rem(my_x - i % 4 + 4, 4)
        cols = slice(g * 256, (g + 1) * 256)
        keys = jnp.concatenate([kvs[a, :, cols], kvs[b, :, cols]], axis=0)
        queries = q_all[slot, :, cols]
        spread = jnp.concatenate([jnp.where(head == h, queries, jnp.zeros_like(queries)) for h in range(4)], axis=0)
        score = lax.dot_general(spread, keys, LAST_DIMS, preferred_element_type=jnp.float32)
        return (score + score * jnp.tanh(score)).astype(jnp.bfloat16)

    def attended(t, g, weight):
        i = work[BLOCK_AT + t]
        p = work[PAIR_AT + t]
        a = work[i * LIST + 2 * p]
        b = work[i * LIST + 2 * p + 1]
        cols = slice(D + g * 256, D + (g + 1) * 256)
        values = jnp.concatenate([kvs[a, :, cols], kvs[b, :, cols]], axis=0)
        every = jnp.dot(weight, values, preferred_element_type=jnp.float32)
        mine = every[:BLK]
        for h in range(1, 4):
            mine = jnp.where(head == h, every[h * BLK : (h + 1) * BLK], mine)
        return mine

    def fill(n, slot):
        for u in range(AT_ONCE):
            for g in range(2):
                held[slot, u, g] = weights(n * AT_ONCE + u, g)

    arrived = ensure(0, jnp.int32(0))
    fill(0, 0)

    def step(n, arrived):
        now = n % 2
        arrived = ensure(n + 1, arrived)
        sums = [attended(n * AT_ONCE + u, g, held[now, u, g]) for u in range(AT_ONCE) for g in range(2)]
        fill(n + 1, 1 - now)
        for u in range(AT_ONCE):
            i = work[BLOCK_AT + n * AT_ONCE + u]
            for g in range(2):
                acc[i, :, g * 256 : (g + 1) * 256] += sums[2 * u + g]
        return arrived

    arrived = lax.fori_loop(0, (work[TOTAL_AT] + AT_ONCE - 1) // AT_ONCE, step, arrived)
    lax.fori_loop(arrived, OWN, arrive, 0)
    for i in range(8):
        for z in range(2):
            for y in range(4):
                first = z * 64 + y * 16
                out_ref[i % 4 * 4 + y, i // 4 * 2 + z] = acc[i, first : first + 16, :].astype(jnp.bfloat16)


def attend(work, queries, own, oth):
    vmem = pl.BlockSpec(memory_space=pltpu.VMEM)
    hbm = pl.BlockSpec(memory_space=pltpu.HBM)
    return pl.pallas_call(
        attend_kernel,
        grid_spec=pltpu.PrefetchScalarGridSpec(
            num_scalar_prefetch=1,
            grid=(),
            in_specs=[vmem] * 8 + [hbm] * 2,
            out_specs=vmem,
            scratch_shapes=[
                pltpu.VMEM((OWN + 1, BLK, 2 * D), jnp.bfloat16),
                pltpu.VMEM((8, BLK, D), jnp.bfloat16),
                pltpu.VMEM((8, BLK, D), jnp.float32),
                pltpu.VMEM((2, AT_ONCE, 2, 4 * BLK, 256), jnp.bfloat16),
                pltpu.SemaphoreType.DMA((OWN,)),
            ],
        ),
        out_shape=jax.ShapeDtypeStruct((16, 4, 16, D), jnp.bfloat16),
        compiler_params=pltpu.CompilerParams(vmem_limit_bytes=52 * 1024 * 1024),
        cost_estimate=pl.CostEstimate(flops=20_000_000_000, bytes_accessed=8_000_000, transcendentals=0),
        name="attend",
    )(work, *queries, own, oth)


def plan_kernel(asked, known, work, used):
    def clear(s, _):
        used[s] = 0
        return 0

    lax.fori_loop(0, SLOTS + 1, clear, 0, unroll=True)
    for k in range(32):
        for core in range(2):
            value = asked[k, core]
            used[jnp.where(value > 0, 2 * value - 2 + core, SLOTS)] = 1

    place = jnp.int32(0)
    for s in range(SLOTS):
        work[SOURCE_AT + place] = s
        work[ROWS_AT + place] = known[8, s]
        place = place + used[s]

    def none(n, _):
        work[SOURCE_AT + n] = 0
        work[ROWS_AT + n] = BLK
        return 0

    lax.fori_loop(place, OWN, none, 0)

    def block(n, counts):
        s = work[SOURCE_AT + n]
        after = []
        for i in range(8):
            work[i * LIST + counts[i]] = n
            after.append(counts[i] + known[i, s])
        return tuple(after)

    counts = lax.fori_loop(0, place, block, (jnp.int32(0),) * 8)
    for i in range(8):
        work[i * LIST + counts[i]] = OWN
        work[i * LIST + OWN] = OWN
        work[i * LIST + OWN + 1] = OWN

    pairs = [(count + 1) // 2 for count in counts]
    most = functools.reduce(jnp.maximum, pairs)

    def level(p, n):
        for i in range(8):
            work[BLOCK_AT + n] = i
            work[PAIR_AT + n] = p
            n = n + (pairs[i] > p).astype(jnp.int32)
        return n

    total = lax.fori_loop(0, most, level, jnp.int32(0))
    for k in range(3 * AT_ONCE):
        work[BLOCK_AT + total + k] = 7
        work[PAIR_AT + total + k] = OWN // 2
    work[TOTAL_AT] = total
    work[TOTAL_AT + 1] = known[9, 0]


def plan(asked, known):
    smem = pl.BlockSpec(memory_space=pltpu.SMEM)
    return pl.pallas_call(
        plan_kernel,
        in_specs=[smem] * 2,
        out_specs=smem,
        out_shape=jax.ShapeDtypeStruct((PLAN,), jnp.int32),
        scratch_shapes=[pltpu.SMEM((SLOTS + 8,), jnp.int32)],
        name="plan",
    )(asked, known)


def on_device(candidates, norm_gain, qu_weight, out_weight, kv_cache, requests, block_mask, hist_len):
    zh, x, zl, y, c = (lax.axis_index(a) for a in AXES)
    first_block = ((zh * 4 + x) * 32 + zl * 8 + y * 2) * OWN
    place = jnp.stack([c, zl * 4 + y]).astype(jnp.int32)

    oth_cache = shift(kv_cache, "c", 1)

    wanted = requests[0]
    holder = wanted // OWN % 32
    to_holder = jnp.sum(
        jnp.where(holder[None, :] == jnp.arange(32)[:, None], wanted[None, :] % OWN + 1, 0), axis=1
    ).reshape(16, 2)
    to_holder = jnp.stack([to_holder, to_holder[:, ::-1]], axis=-1).reshape(32, 2)
    asked = lax.all_to_all(to_holder, HIST, 0, 0, tiled=True)

    rows = lax.dynamic_slice_in_dim(candidates, c * BLK, BLK, 0)
    across = shift(rows, "zh", 1)
    across, asked = lax.optimization_barrier((across, asked))
    near, far = project(rows, across, norm_gain, qu_weight)
    near_1, far_1, near_3, far_3 = shift(near, "x", 1), shift(far, "x", 1), shift(near, "x", -1), shift(far, "x", -1)
    near_2, far_2 = shift(near_1, "x", 1), shift(far_3, "x", -1)
    queries = (near, near_1, near_2, near_3, far, far_1, far_2, far_3)

    lens = lax.dynamic_slice_in_dim(hist_len, first_block, SLOTS, 0).reshape(2, OWN)
    lens = jnp.where(c == 0, lens, lens[::-1]).T.reshape(SLOTS)
    mask = lax.dynamic_slice_in_dim(block_mask, first_block, SLOTS, 1).reshape(2, 4, 2, 2, OWN)
    mask = lax.dynamic_index_in_dim(mask, c, 2, keepdims=False)
    mask = jnp.where(c == 0, mask, mask[:, :, ::-1])
    mask = jnp.where(zh == 0, mask, mask[::-1]).swapaxes(2, 3).reshape(8, SLOTS)
    known = jnp.concatenate([mask, lens[None], jnp.broadcast_to(x, (1, SLOTS))])
    sums = attend(plan(asked, known), queries, kv_cache, oth_cache)

    parts = lax.all_to_all(sums.reshape(16, 64, D), ("x", "y"), 0, 0, tiled=True)
    sums = jnp.sum(parts.astype(jnp.float32), axis=0).astype(jnp.bfloat16).reshape(2, 1, 1, 4, 8, D)

    own_zh = jnp.arange(2)[:, None, None, None, None] == zh
    own_parity = jnp.arange(2)[None, :, None, None, None] == c
    sums = jnp.where(own_parity, jnp.where(own_zh, sums[0], sums[1]), jnp.bfloat16(0))
    parts = lax.all_to_all(sums.reshape(16, 8, D), ("zh", "zl", "c"), 0, 0, tiled=True)
    gate = project_gate(place, candidates, norm_gain, qu_weight)
    return finish(place, parts, gate, candidates, out_weight)


def solution(mesh):
    fine = Mesh(mesh.devices.reshape(2, 4, 4, 4, 2), AXES)
    placed = (
        P(CAND, None),
        P(),
        P(),
        P(),
        P(AXES, None, None),
        P(AXES, None),
        P(),
        P(),
    )
    return jax.shard_map(on_device, mesh=fine, in_specs=placed, out_specs=P(AXES, None), check_vma=False)
```

```python
import functools

import jax
import jax.numpy as jnp
from jax import lax
from jax.experimental import pallas as pl
from jax.experimental.pallas import tpu as pltpu
from jax.sharding import Mesh, PartitionSpec as P

H = 8
DH = 64
D = H * DH
BLK = 128
OWN = 32
EPS = 1e-05
HALF_SCALE = 0.0625
LAST_DIMS = (((1,), (1,)), ((), ()))
AXES = ("zh", "x", "zl", "y", "c")
CAND = ("zh", "x")
HIST = ("zl", "y", "c")
SLOTS = 2 * OWN
AT_ONCE = 3
ITEMS = 4 * OWN + 4 * AT_ONCE
LIST = OWN + 4
BLOCK_AT = 8 * LIST
PAIR_AT = BLOCK_AT + ITEMS
SOURCE_AT = PAIR_AT + ITEMS
ROWS_AT = SOURCE_AT + OWN + 8
TOTAL_AT = ROWS_AT + OWN + 8
PLAN = TOTAL_AT + 8


PROJECT_VMEM = 54016 * 1024
ATTEND_VMEM = 53760 * 1024


def normalize_input(values, norm_gain):
    center = jnp.mean(values, axis=-1, keepdims=True)
    spread = jnp.mean(jnp.square(values - center), axis=-1, keepdims=True)
    return ((values - center) * lax.rsqrt(spread + EPS) * norm_gain).astype(jnp.bfloat16)


def silu(values):
    half = 0.5 * values
    return half + half * jnp.tanh(half)


def shift(value, axis, steps):
    count = lax.axis_size(axis)
    return lax.ppermute(value, axis, [(i, (i + steps) % count) for i in range(count)])


def project_kernel(near_rows, far_rows, gain_hbm, weight_hbm, near_ref, far_ref, gain, weight, sem):
    copies = [
        pltpu.make_async_copy(gain_hbm, gain, sem.at[0]),
        pltpu.make_async_copy(weight_hbm.at[:, pl.ds(0, D)], weight, sem.at[1]),
    ]
    for copy in copies:
        copy.start()
    rows = jnp.concatenate([near_rows[...], far_rows[...]], axis=0).astype(jnp.float32)
    copies[0].wait()
    normed = normalize_input(rows, gain[...])
    copies[1].wait()
    projected = jnp.dot(normed, weight[...], preferred_element_type=jnp.float32)
    queries = silu(projected).astype(jnp.bfloat16) * jnp.bfloat16(HALF_SCALE)
    near_ref[...] = queries[:BLK]
    far_ref[...] = queries[BLK:]


def project(near, far, norm_gain, qu_weight):
    vmem = pl.BlockSpec(memory_space=pltpu.VMEM)
    hbm = pl.BlockSpec(memory_space=pltpu.HBM)
    return pl.pallas_call(
        project_kernel,
        in_specs=[vmem] * 2 + [hbm] * 2,
        out_specs=[vmem] * 2,
        scratch_shapes=[
            pltpu.VMEM((1, D), jnp.float32),
            pltpu.VMEM((D, D), jnp.bfloat16),
            pltpu.SemaphoreType.DMA((2,)),
        ],
        out_shape=[jax.ShapeDtypeStruct((BLK, D), jnp.bfloat16)] * 2,
        compiler_params=pltpu.CompilerParams(vmem_limit_bytes=PROJECT_VMEM),
        name="project",
    )(near, far, norm_gain.reshape(1, D), qu_weight)


def output_rows():
    return pl.ds(pl.multiple_of((lax.axis_index("zl") * 4 + lax.axis_index("y")) * 16, 16), 16)


def gate_kernel(cand_ref, gain_ref, weight_ref, gate_ref):
    rows = cand_ref[output_rows(), :].astype(jnp.float32)
    normed = normalize_input(rows, gain_ref[...])
    gate_ref[...] = silu(jnp.dot(normed, weight_ref[:, D:], preferred_element_type=jnp.float32))


def project_gate(candidates, norm_gain, qu_weight):
    vmem = pl.BlockSpec(memory_space=pltpu.VMEM)
    return pl.pallas_call(
        gate_kernel,
        in_specs=[vmem] * 3,
        out_specs=vmem,
        out_shape=jax.ShapeDtypeStruct((16, D), jnp.float32),
        compiler_params=pltpu.CompilerParams(vmem_limit_bytes=16 * 1024 * 1024),
        name="gate",
    )(candidates, norm_gain.reshape(1, D), qu_weight)


def finish_kernel(parts_ref, gate_ref, cand_ref, weight_ref, out_ref):
    summed = jnp.sum(parts_ref[...].astype(jnp.float32), axis=0)
    core = lax.axis_index("c")
    gate = jnp.where(core == 0, gate_ref[:8], gate_ref[8:])
    rows = cand_ref[output_rows(), :].astype(jnp.float32)
    rows = jnp.where(core == 0, rows[:8], rows[8:])
    heads = []
    for h in range(H):
        one = summed[:, h * DH : (h + 1) * DH]
        center = jnp.mean(one, axis=-1, keepdims=True)
        spread = jnp.mean(jnp.square(one - center), axis=-1, keepdims=True)
        heads.append((one - center) * lax.rsqrt(spread + EPS))
    mixed = (jnp.concatenate(heads, axis=1) * gate).astype(jnp.bfloat16)
    output = rows + jnp.dot(mixed, weight_ref[...], preferred_element_type=jnp.float32)
    out_ref[...] = output.astype(jnp.bfloat16)


def finish(parts, gate, candidates, out_weight):
    vmem = pl.BlockSpec(memory_space=pltpu.VMEM)
    return pl.pallas_call(
        finish_kernel,
        in_specs=[vmem] * 4,
        out_specs=vmem,
        out_shape=jax.ShapeDtypeStruct((8, D), jnp.bfloat16),
        compiler_params=pltpu.CompilerParams(vmem_limit_bytes=16 * 1024 * 1024),
        name="finish",
    )(parts, gate, candidates, out_weight)


def fetch_used(asked, work, used, own_ref, oth_ref, kvs, sem):
    for s in range(SLOTS + 1):
        used[s] = 0
    for k in range(32):
        for other in range(2):
            value = asked[k, 0, other]
            used[jnp.where(value > 0, 2 * value - 2 + other, SLOTS)] = 1

    def start(s, place):
        for other, ref in enumerate((own_ref, oth_ref)):
            work[SOURCE_AT + place] = 2 * s + other

            @pl.when(used[2 * s + other] > 0)
            def _(place=place, ref=ref):
                pltpu.make_async_copy(ref.at[s], kvs.at[place], sem.at[place]).start()

            place = place + used[2 * s + other]
        return place

    return lax.fori_loop(0, OWN, start, jnp.int32(0))


def list_items(mask, lens, first, count, work):
    core, zh = lax.axis_index("c"), lax.axis_index("zh")
    columns = [first + core * OWN, first + (1 - core) * OWN]
    rows = [(jnp.bitwise_xor(zh, i // 4) * 4 + i % 4) * 2 + core for i in range(8)]

    def block(n, counts):
        s = work[SOURCE_AT + n]
        column = jnp.where(s % 2 == 0, columns[0], columns[1]) + s // 2
        work[ROWS_AT + n] = lens[0, column]
        after = []
        for i in range(8):
            work[i * LIST + counts[i]] = n
            after.append(counts[i] + mask[rows[i], column])
        return tuple(after)

    counts = lax.fori_loop(0, count, block, (jnp.int32(0),) * 8)
    for i in range(8):
        work[i * LIST + counts[i]] = OWN
        work[i * LIST + OWN] = OWN
        work[i * LIST + OWN + 1] = OWN

    pairs = [(counts[i] + 1) // 2 for i in range(8)]
    most = functools.reduce(jnp.maximum, pairs)

    def level(p, n):
        for i in range(8):
            work[BLOCK_AT + n] = i
            work[PAIR_AT + n] = p
            n = n + (pairs[i] > p).astype(jnp.int32)
        return n

    total = lax.fori_loop(0, most, level, jnp.int32(0))
    for k in range(3 * AT_ONCE):
        work[BLOCK_AT + total + k] = 7
        work[PAIR_AT + total + k] = OWN // 2
    return total


def attend_kernel(asked, mask_hbm, lens_hbm, *rest):
    *q_refs, own_ref, oth_ref, out_ref, kvs, q_all, acc, held, sem, work, used, mask, lens, known_sem = rest
    chip = ((lax.axis_index("zh") * 4 + lax.axis_index("x")) * 4 + lax.axis_index("zl")) * 4 + lax.axis_index("y")
    aligned = pl.multiple_of(chip // 2 * 128, 128)
    known = [
        pltpu.make_async_copy(mask_hbm.at[:, pl.ds(aligned, 128)], mask, known_sem.at[0]),
        pltpu.make_async_copy(lens_hbm.at[pl.ds(chip // 2, 1), :], lens, known_sem.at[1]),
    ]
    for copy in known:
        copy.start()
    count = fetch_used(asked, work, used, own_ref, oth_ref, kvs, sem)
    for copy in known:
        copy.wait()
    total = list_items(mask, lens, chip % 2 * SLOTS, count, work)
    kvs[OWN] = jnp.zeros((BLK, 2 * D), jnp.bfloat16)
    acc[...] = jnp.zeros_like(acc)
    for k, ref in enumerate(q_refs):
        q_all[k] = ref[...]

    def arrive(k, _):
        pltpu.make_async_copy(own_ref.at[0], kvs.at[k], sem.at[k]).wait()

        @pl.when(work[ROWS_AT + k] < BLK)
        def _():
            row = lax.broadcasted_iota(jnp.int32, (BLK, D), 0)
            values = kvs[k, :, D:].astype(jnp.float32)
            kvs[k, :, D:] = jnp.where(row < work[ROWS_AT + k], values, 0.0).astype(jnp.bfloat16)

        return 0

    def ensure(n, arrived):
        upto = arrived
        for u in range(AT_ONCE):
            i = work[BLOCK_AT + n * AT_ONCE + u]
            p = work[PAIR_AT + n * AT_ONCE + u]
            for part in range(2):
                block = work[i * LIST + 2 * p + part]
                upto = jnp.maximum(upto, jnp.where(block < OWN, block + 1, 0))
        lax.fori_loop(arrived, upto, arrive, 0)
        return upto

    head = lax.broadcasted_iota(jnp.int32, (BLK, 256), 1) // DH
    my_x = lax.axis_index("x")

    def weights(t, g):
        i = work[BLOCK_AT + t]
        p = work[PAIR_AT + t]
        a = work[i * LIST + 2 * p]
        b = work[i * LIST + 2 * p + 1]
        slot = i // 4 * 4 + lax.rem(my_x - i % 4 + 4, 4)
        cols = slice(g * 256, (g + 1) * 256)
        keys = jnp.concatenate([kvs[a, :, cols], kvs[b, :, cols]], axis=0)
        queries = q_all[slot, :, cols]
        spread = jnp.concatenate([jnp.where(head == h, queries, jnp.zeros_like(queries)) for h in range(4)], axis=0)
        score = lax.dot_general(spread, keys, LAST_DIMS, preferred_element_type=jnp.float32)
        return (score + score * jnp.tanh(score)).astype(jnp.bfloat16)

    def attended(t, g, weight):
        i = work[BLOCK_AT + t]
        p = work[PAIR_AT + t]
        a = work[i * LIST + 2 * p]
        b = work[i * LIST + 2 * p + 1]
        cols = slice(D + g * 256, D + (g + 1) * 256)
        values = jnp.concatenate([kvs[a, :, cols], kvs[b, :, cols]], axis=0)
        every = jnp.dot(weight, values, preferred_element_type=jnp.float32)
        mine = every[:BLK]
        for h in range(1, 4):
            mine = jnp.where(head == h, every[h * BLK : (h + 1) * BLK], mine)
        return mine

    def fill(n, slot):
        for u in range(AT_ONCE):
            for g in range(2):
                held[slot, u, g] = weights(n * AT_ONCE + u, g)

    arrived = ensure(0, jnp.int32(0))
    fill(0, 0)

    def step(n, arrived):
        now = n % 2
        arrived = ensure(n + 1, arrived)
        sums = [attended(n * AT_ONCE + u, g, held[now, u, g]) for u in range(AT_ONCE) for g in range(2)]
        fill(n + 1, 1 - now)
        for u in range(AT_ONCE):
            i = work[BLOCK_AT + n * AT_ONCE + u]
            for g in range(2):
                acc[i, :, g * 256 : (g + 1) * 256] += sums[2 * u + g]
        return arrived

    arrived = lax.fori_loop(0, (total + AT_ONCE - 1) // AT_ONCE, step, arrived)
    lax.fori_loop(arrived, count, arrive, 0)
    for i in range(8):
        for z in range(2):
            for y in range(4):
                first = z * 64 + y * 16
                out_ref[i % 4 * 4 + y, i // 4 * 2 + z] = acc[i, first : first + 16, :].astype(jnp.bfloat16)


def attend(scalars, queries, own, oth):
    smem = pl.BlockSpec(memory_space=pltpu.SMEM)
    vmem = pl.BlockSpec(memory_space=pltpu.VMEM)
    hbm = pl.BlockSpec(memory_space=pltpu.HBM)
    return pl.pallas_call(
        attend_kernel,
        in_specs=[smem] + [hbm] * 2 + [vmem] * 8 + [hbm] * 2,
        out_specs=vmem,
        scratch_shapes=[
            pltpu.VMEM((OWN + 1, BLK, 2 * D), jnp.bfloat16),
            pltpu.VMEM((8, BLK, D), jnp.bfloat16),
            pltpu.VMEM((8, BLK, D), jnp.float32),
            pltpu.VMEM((2, AT_ONCE, 2, 4 * BLK, 256), jnp.bfloat16),
            pltpu.SemaphoreType.DMA((OWN,)),
            pltpu.SMEM((PLAN,), jnp.int32),
            pltpu.SMEM((SLOTS + 8,), jnp.int32),
            pltpu.SMEM((16, 128), jnp.int32),
            pltpu.SMEM((1, 128), jnp.int32),
            pltpu.SemaphoreType.DMA((2,)),
        ],
        out_shape=jax.ShapeDtypeStruct((16, 4, 16, D), jnp.bfloat16),
        compiler_params=pltpu.CompilerParams(vmem_limit_bytes=ATTEND_VMEM),
        cost_estimate=pl.CostEstimate(flops=20_000_000_000, bytes_accessed=8_000_000, transcendentals=0),
        name="attend",
    )(*scalars, *queries, own, oth)


def place_sums_kernel(parts_ref, out_ref):
    core, zh = lax.axis_index("c"), lax.axis_index("zh")
    sums = jnp.sum(parts_ref[...].astype(jnp.float32), axis=0)
    near, far = sums[:32], sums[32:]
    halves = [jnp.where(zh == 0, near, far), jnp.where(zh == 0, far, near)]
    for z in range(2):
        for parity in range(2):
            mine = jnp.where(core == parity, halves[z], 0.0).astype(jnp.bfloat16)
            for k in range(4):
                out_ref[z * 8 + parity * 4 + k] = mine[k * 8 : (k + 1) * 8]


def place_sums(parts):
    vmem = pl.BlockSpec(memory_space=pltpu.VMEM)
    return pl.pallas_call(
        place_sums_kernel,
        in_specs=[vmem],
        out_specs=vmem,
        out_shape=jax.ShapeDtypeStruct((16, 8, D), jnp.bfloat16),
        compiler_params=pltpu.CompilerParams(vmem_limit_bytes=16 * 1024 * 1024),
        name="place_sums",
    )(parts)


def on_device(candidates, norm_gain, qu_weight, out_weight, kv_cache, requests, block_mask, hist_len):
    oth_cache = shift(kv_cache, "c", 1)

    wanted = requests[0]
    asker = jnp.bitwise_xor(jnp.arange(32)[:, None, None, None], jnp.arange(128)[None, None, :, None])
    to_holder = jnp.sum(jnp.where(wanted // OWN % 32 == asker, wanted % OWN + 1, 0), axis=3)
    asked = lax.all_to_all(to_holder, HIST, 0, 0, tiled=True)

    rows = lax.dynamic_slice_in_dim(candidates, lax.axis_index("c") * BLK, BLK, 0)
    across = shift(rows, "zh", 1)
    across, asked = lax.optimization_barrier((across, asked))
    near, far = project(rows, across, norm_gain, qu_weight)
    near_1, far_1, near_3, far_3 = shift(near, "x", 1), shift(far, "x", 1), shift(near, "x", -1), shift(far, "x", -1)
    near_2, far_2 = shift(near_1, "x", 1), shift(far_3, "x", -1)
    queries = (near, near_1, near_2, near_3, far, far_1, far_2, far_3)

    sums = attend((asked, block_mask, hist_len.reshape(-1, 128)), queries, kv_cache, oth_cache)

    parts = lax.all_to_all(sums.reshape(16, 64, D), ("x", "y"), 0, 0, tiled=True)
    parts = lax.all_to_all(place_sums(parts), ("zh", "zl", "c"), 0, 0, tiled=True)
    gate = project_gate(candidates, norm_gain, qu_weight)
    return finish(parts, gate, candidates, out_weight)


def solution(mesh):
    fine = Mesh(mesh.devices.reshape(2, 4, 4, 4, 2), AXES)
    placed = (
        P(CAND, None),
        P(),
        P(),
        P(),
        P(AXES, None, None),
        P(AXES, None),
        P(),
        P(),
    )
    return jax.shard_map(on_device, mesh=fine, in_specs=placed, out_specs=P(AXES, None), check_vma=False)
```

```python
import functools

import jax
import jax.numpy as jnp
from jax import lax
from jax.experimental import pallas as pl
from jax.experimental.pallas import tpu as pltpu
from jax.sharding import Mesh, PartitionSpec as P

H = 8
DH = 64
D = H * DH
BLK = 128
OWN = 32
EPS = 1e-05
HALF_SCALE = 0.0625
LAST_DIMS = (((1,), (1,)), ((), ()))
AXES = ("zh", "x", "zl", "y", "c")
CAND = ("zh", "x")
HIST = ("zl", "y", "c")
SLOTS = 2 * OWN
AT_ONCE = 3
ITEMS = 4 * OWN + 4 * AT_ONCE
LIST = OWN + 4
BLOCK_AT = 8 * LIST
PAIR_AT = BLOCK_AT + ITEMS
SOURCE_AT = PAIR_AT + ITEMS
ROWS_AT = SOURCE_AT + OWN + 8
TOTAL_AT = ROWS_AT + OWN + 8
PLAN = TOTAL_AT + 8


PROJECT_VMEM = 54016 * 1024
ATTEND_VMEM = 53760 * 1024


def normalize_input(values, norm_gain):
    center = jnp.mean(values, axis=-1, keepdims=True)
    spread = jnp.mean(jnp.square(values - center), axis=-1, keepdims=True)
    return ((values - center) * lax.rsqrt(spread + EPS) * norm_gain).astype(jnp.bfloat16)


def silu(values):
    half = 0.5 * values
    return half + half * jnp.tanh(half)


def shift(value, axis, steps):
    count = lax.axis_size(axis)
    return lax.ppermute(value, axis, [(i, (i + steps) % count) for i in range(count)])


def project_kernel(near_rows, far_rows, gain_hbm, weight_hbm, near_ref, far_ref, gain, weight, sem):
    copies = [
        pltpu.make_async_copy(gain_hbm, gain, sem.at[0]),
        pltpu.make_async_copy(weight_hbm.at[:, pl.ds(0, D)], weight, sem.at[1]),
    ]
    for copy in copies:
        copy.start()
    rows = jnp.concatenate([near_rows[...], far_rows[...]], axis=0).astype(jnp.float32)
    copies[0].wait()
    normed = normalize_input(rows, gain[...])
    copies[1].wait()
    projected = jnp.dot(normed, weight[...], preferred_element_type=jnp.float32)
    queries = silu(projected).astype(jnp.bfloat16) * jnp.bfloat16(HALF_SCALE)
    near_ref[...] = queries[:BLK]
    far_ref[...] = queries[BLK:]


def project(near, far, norm_gain, qu_weight):
    vmem = pl.BlockSpec(memory_space=pltpu.VMEM)
    hbm = pl.BlockSpec(memory_space=pltpu.HBM)
    return pl.pallas_call(
        project_kernel,
        in_specs=[vmem] * 2 + [hbm] * 2,
        out_specs=[vmem] * 2,
        scratch_shapes=[
            pltpu.VMEM((1, D), jnp.float32),
            pltpu.VMEM((D, D), jnp.bfloat16),
            pltpu.SemaphoreType.DMA((2,)),
        ],
        out_shape=[jax.ShapeDtypeStruct((BLK, D), jnp.bfloat16)] * 2,
        compiler_params=pltpu.CompilerParams(vmem_limit_bytes=PROJECT_VMEM),
        name="project",
    )(near, far, norm_gain.reshape(1, D), qu_weight)


def output_rows():
    return pl.ds(pl.multiple_of((lax.axis_index("zl") * 4 + lax.axis_index("y")) * 16, 16), 16)


def gate_kernel(cand_ref, gain_ref, weight_ref, gate_ref):
    rows = cand_ref[output_rows(), :].astype(jnp.float32)
    normed = normalize_input(rows, gain_ref[...])
    gate_ref[...] = silu(jnp.dot(normed, weight_ref[:, D:], preferred_element_type=jnp.float32))


def project_gate(candidates, norm_gain, qu_weight):
    vmem = pl.BlockSpec(memory_space=pltpu.VMEM)
    return pl.pallas_call(
        gate_kernel,
        in_specs=[vmem] * 3,
        out_specs=vmem,
        out_shape=jax.ShapeDtypeStruct((16, D), jnp.float32),
        compiler_params=pltpu.CompilerParams(vmem_limit_bytes=16 * 1024 * 1024),
        name="gate",
    )(candidates, norm_gain.reshape(1, D), qu_weight)


def finish_kernel(parts_ref, gate_ref, cand_ref, weight_ref, out_ref):
    summed = jnp.sum(parts_ref[...].astype(jnp.float32), axis=0)
    core = lax.axis_index("c")
    gate = jnp.where(core == 0, gate_ref[:8], gate_ref[8:])
    rows = cand_ref[output_rows(), :].astype(jnp.float32)
    rows = jnp.where(core == 0, rows[:8], rows[8:])
    heads = []
    for h in range(H):
        one = summed[:, h * DH : (h + 1) * DH]
        center = jnp.mean(one, axis=-1, keepdims=True)
        spread = jnp.mean(jnp.square(one - center), axis=-1, keepdims=True)
        heads.append((one - center) * lax.rsqrt(spread + EPS))
    mixed = (jnp.concatenate(heads, axis=1) * gate).astype(jnp.bfloat16)
    output = rows + jnp.dot(mixed, weight_ref[...], preferred_element_type=jnp.float32)
    out_ref[...] = output.astype(jnp.bfloat16)


def finish(parts, gate, candidates, out_weight):
    vmem = pl.BlockSpec(memory_space=pltpu.VMEM)
    return pl.pallas_call(
        finish_kernel,
        in_specs=[vmem] * 4,
        out_specs=vmem,
        out_shape=jax.ShapeDtypeStruct((8, D), jnp.bfloat16),
        compiler_params=pltpu.CompilerParams(vmem_limit_bytes=16 * 1024 * 1024),
        name="finish",
    )(parts, gate, candidates, out_weight)


def fetch_used(requests, first, work, used, own_ref, oth_ref, kvs, sem):
    for s in range(SLOTS + 1):
        used[s] = 0
    core = lax.axis_index("c")
    base = first - core * OWN
    for ref in requests:

        def mark(r, _, ref=ref):
            for k in range(16):
                block = ref[r, k] - base
                slot = ((block & (OWN - 1)) << 1) | ((block >> 5) ^ core)
                used[jnp.where(block >> 6 == 0, slot, SLOTS)] = 1
            return 0

        lax.fori_loop(0, 8, mark, 0, unroll=True)

    def start(s, place):
        for other, ref in enumerate((own_ref, oth_ref)):
            work[SOURCE_AT + place] = 2 * s + other

            @pl.when(used[2 * s + other] > 0)
            def _(place=place, ref=ref):
                pltpu.make_async_copy(ref.at[s], kvs.at[place], sem.at[place]).start()

            place = place + used[2 * s + other]
        return place

    return lax.fori_loop(0, OWN, start, jnp.int32(0))


def list_items(mask, lens, first, count, work):
    core, zh = lax.axis_index("c"), lax.axis_index("zh")
    columns = [first + core * OWN, first + (1 - core) * OWN]
    rows = [(jnp.bitwise_xor(zh, i // 4) * 4 + i % 4) * 2 + core for i in range(8)]

    def block(n, counts):
        s = work[SOURCE_AT + n]
        column = jnp.where(s % 2 == 0, columns[0], columns[1]) + s // 2
        work[ROWS_AT + n] = lens[0, column]
        after = []
        for i in range(8):
            work[i * LIST + counts[i]] = n
            after.append(counts[i] + mask[rows[i], column])
        return tuple(after)

    counts = lax.fori_loop(0, count, block, (jnp.int32(0),) * 8)
    for i in range(8):
        work[i * LIST + counts[i]] = OWN
        work[i * LIST + OWN] = OWN
        work[i * LIST + OWN + 1] = OWN

    pairs = [(counts[i] + 1) // 2 for i in range(8)]
    most = functools.reduce(jnp.maximum, pairs)

    def level(p, n):
        for i in range(8):
            work[BLOCK_AT + n] = i
            work[PAIR_AT + n] = p
            n = n + (pairs[i] > p).astype(jnp.int32)
        return n

    total = lax.fori_loop(0, most, level, jnp.int32(0))
    for k in range(3 * AT_ONCE):
        work[BLOCK_AT + total + k] = 7
        work[PAIR_AT + total + k] = OWN // 2
    return total


def attend_kernel(r0, r1, r2, r3, mask_hbm, lens_hbm, *rest):
    *q_refs, own_ref, oth_ref, out_ref, kvs, q_all, acc, held, sem, work, used, mask, lens, known_sem = rest
    chip = ((lax.axis_index("zh") * 4 + lax.axis_index("x")) * 4 + lax.axis_index("zl")) * 4 + lax.axis_index("y")
    aligned = pl.multiple_of(chip // 2 * 128, 128)
    known = [
        pltpu.make_async_copy(mask_hbm.at[:, pl.ds(aligned, 128)], mask, known_sem.at[0]),
        pltpu.make_async_copy(lens_hbm.at[pl.ds(chip // 2, 1), :], lens, known_sem.at[1]),
    ]
    for copy in known:
        copy.start()
    first = (2 * chip + lax.axis_index("c")) * OWN
    count = fetch_used((r0, r1, r2, r3), first, work, used, own_ref, oth_ref, kvs, sem)
    for copy in known:
        copy.wait()
    total = list_items(mask, lens, chip % 2 * SLOTS, count, work)
    kvs[OWN] = jnp.zeros((BLK, 2 * D), jnp.bfloat16)
    acc[...] = jnp.zeros_like(acc)
    for k, ref in enumerate(q_refs):
        q_all[k] = ref[...]

    def arrive(k, _):
        pltpu.make_async_copy(own_ref.at[0], kvs.at[k], sem.at[k]).wait()

        @pl.when(work[ROWS_AT + k] < BLK)
        def _():
            row = lax.broadcasted_iota(jnp.int32, (BLK, D), 0)
            values = kvs[k, :, D:].astype(jnp.float32)
            kvs[k, :, D:] = jnp.where(row < work[ROWS_AT + k], values, 0.0).astype(jnp.bfloat16)

        return 0

    def ensure(n, arrived):
        upto = arrived
        for u in range(AT_ONCE):
            i = work[BLOCK_AT + n * AT_ONCE + u]
            p = work[PAIR_AT + n * AT_ONCE + u]
            for part in range(2):
                block = work[i * LIST + 2 * p + part]
                upto = jnp.maximum(upto, jnp.where(block < OWN, block + 1, 0))
        lax.fori_loop(arrived, upto, arrive, 0)
        return upto

    head = lax.broadcasted_iota(jnp.int32, (BLK, 256), 1) // DH
    my_x = lax.axis_index("x")

    def weights(t, g):
        i = work[BLOCK_AT + t]
        p = work[PAIR_AT + t]
        a = work[i * LIST + 2 * p]
        b = work[i * LIST + 2 * p + 1]
        slot = i // 4 * 4 + lax.rem(my_x - i % 4 + 4, 4)
        cols = slice(g * 256, (g + 1) * 256)
        keys = jnp.concatenate([kvs[a, :, cols], kvs[b, :, cols]], axis=0)
        queries = q_all[slot, :, cols]
        spread = jnp.concatenate([jnp.where(head == h, queries, jnp.zeros_like(queries)) for h in range(4)], axis=0)
        score = lax.dot_general(spread, keys, LAST_DIMS, preferred_element_type=jnp.float32)
        return (score + score * jnp.tanh(score)).astype(jnp.bfloat16)

    def attended(t, g, weight):
        i = work[BLOCK_AT + t]
        p = work[PAIR_AT + t]
        a = work[i * LIST + 2 * p]
        b = work[i * LIST + 2 * p + 1]
        cols = slice(D + g * 256, D + (g + 1) * 256)
        values = jnp.concatenate([kvs[a, :, cols], kvs[b, :, cols]], axis=0)
        every = jnp.dot(weight, values, preferred_element_type=jnp.float32)
        mine = every[:BLK]
        for h in range(1, 4):
            mine = jnp.where(head == h, every[h * BLK : (h + 1) * BLK], mine)
        return mine

    def fill(n, slot):
        for u in range(AT_ONCE):
            for g in range(2):
                held[slot, u, g] = weights(n * AT_ONCE + u, g)

    arrived = ensure(0, jnp.int32(0))
    fill(0, 0)

    def step(n, arrived):
        now = n % 2
        arrived = ensure(n + 1, arrived)
        sums = [attended(n * AT_ONCE + u, g, held[now, u, g]) for u in range(AT_ONCE) for g in range(2)]
        fill(n + 1, 1 - now)
        for u in range(AT_ONCE):
            i = work[BLOCK_AT + n * AT_ONCE + u]
            for g in range(2):
                acc[i, :, g * 256 : (g + 1) * 256] += sums[2 * u + g]
        return arrived

    arrived = lax.fori_loop(0, (total + AT_ONCE - 1) // AT_ONCE, step, arrived)
    lax.fori_loop(arrived, count, arrive, 0)
    for i in range(8):
        for z in range(2):
            for y in range(4):
                first = z * 64 + y * 16
                out_ref[i % 4 * 4 + y, i // 4 * 2 + z] = acc[i, first : first + 16, :].astype(jnp.bfloat16)


def attend(scalars, queries, own, oth):
    smem = pl.BlockSpec(memory_space=pltpu.SMEM)
    vmem = pl.BlockSpec(memory_space=pltpu.VMEM)
    hbm = pl.BlockSpec(memory_space=pltpu.HBM)
    return pl.pallas_call(
        attend_kernel,
        in_specs=[smem] * 4 + [hbm] * 2 + [vmem] * 8 + [hbm] * 2,
        out_specs=vmem,
        scratch_shapes=[
            pltpu.VMEM((OWN + 1, BLK, 2 * D), jnp.bfloat16),
            pltpu.VMEM((8, BLK, D), jnp.bfloat16),
            pltpu.VMEM((8, BLK, D), jnp.float32),
            pltpu.VMEM((2, AT_ONCE, 2, 4 * BLK, 256), jnp.bfloat16),
            pltpu.SemaphoreType.DMA((OWN,)),
            pltpu.SMEM((PLAN,), jnp.int32),
            pltpu.SMEM((SLOTS + 8,), jnp.int32),
            pltpu.SMEM((16, 128), jnp.int32),
            pltpu.SMEM((1, 128), jnp.int32),
            pltpu.SemaphoreType.DMA((2,)),
        ],
        out_shape=jax.ShapeDtypeStruct((16, 4, 16, D), jnp.bfloat16),
        compiler_params=pltpu.CompilerParams(vmem_limit_bytes=ATTEND_VMEM),
        cost_estimate=pl.CostEstimate(flops=20_000_000_000, bytes_accessed=8_000_000, transcendentals=0),
        name="attend",
    )(*scalars, *queries, own, oth)


def place_sums_kernel(parts_ref, out_ref):
    core, zh = lax.axis_index("c"), lax.axis_index("zh")
    sums = jnp.sum(parts_ref[...].astype(jnp.float32), axis=0)
    near, far = sums[:32], sums[32:]
    halves = [jnp.where(zh == 0, near, far), jnp.where(zh == 0, far, near)]
    for z in range(2):
        for parity in range(2):
            mine = jnp.where(core == parity, halves[z], 0.0).astype(jnp.bfloat16)
            for k in range(4):
                out_ref[z * 8 + parity * 4 + k] = mine[k * 8 : (k + 1) * 8]


def place_sums(parts):
    vmem = pl.BlockSpec(memory_space=pltpu.VMEM)
    return pl.pallas_call(
        place_sums_kernel,
        in_specs=[vmem],
        out_specs=vmem,
        out_shape=jax.ShapeDtypeStruct((16, 8, D), jnp.bfloat16),
        compiler_params=pltpu.CompilerParams(vmem_limit_bytes=16 * 1024 * 1024),
        name="place_sums",
    )(parts)


def on_device(candidates, norm_gain, qu_weight, out_weight, kv_cache, requests, block_mask, hist_len):
    oth_cache = shift(kv_cache, "c", 1)

    rows = lax.dynamic_slice_in_dim(candidates, lax.axis_index("c") * BLK, BLK, 0)
    across = shift(rows, "zh", 1)
    asked = jnp.concatenate([requests, shift(requests, "c", 1)])
    across, asked = lax.optimization_barrier((across, asked))
    asked = jnp.concatenate([asked] + [shift(asked, "y", s) for s in range(1, 4)])
    asked = [asked] + [shift(asked, "zl", s) for s in range(1, 4)]
    near, far = project(rows, across, norm_gain, qu_weight)
    near_1, far_1, near_3, far_3 = shift(near, "x", 1), shift(far, "x", 1), shift(near, "x", -1), shift(far, "x", -1)
    near_2, far_2 = shift(near_1, "x", 1), shift(far_3, "x", -1)
    queries = (near, near_1, near_2, near_3, far, far_1, far_2, far_3)

    sums = attend((*asked, block_mask, hist_len.reshape(-1, 128)), queries, kv_cache, oth_cache)

    parts = lax.all_to_all(sums.reshape(16, 64, D), ("x", "y"), 0, 0, tiled=True)
    parts = lax.all_to_all(place_sums(parts), ("zh", "zl", "c"), 0, 0, tiled=True)
    gate = project_gate(candidates, norm_gain, qu_weight)
    return finish(parts, gate, candidates, out_weight)


def solution(mesh):
    fine = Mesh(mesh.devices.reshape(2, 4, 4, 4, 2), AXES)
    placed = (
        P(CAND, None),
        P(),
        P(),
        P(),
        P(AXES, None, None),
        P(AXES, None),
        P(),
        P(),
    )
    return jax.shard_map(on_device, mesh=fine, in_specs=placed, out_specs=P(AXES, None), check_vma=False)
```

```python
import functools

import jax
import jax.numpy as jnp
from jax import lax
from jax.experimental import pallas as pl
from jax.experimental.pallas import tpu as pltpu
from jax.sharding import Mesh, PartitionSpec as P

H = 8
DH = 64
D = H * DH
BLK = 128
OWN = 32
EPS = 1e-05
HALF_SCALE = 0.0625
LAST_DIMS = (((1,), (1,)), ((), ()))
AXES = ("zh", "x", "zl", "y", "c")
CAND = ("zh", "x")
HIST = ("zl", "y", "c")
SLOTS = 2 * OWN
AT_ONCE = 3
ITEMS = 4 * OWN + 4 * AT_ONCE
LIST = OWN + 4
BLOCK_AT = 8 * LIST
PAIR_AT = BLOCK_AT + ITEMS
SOURCE_AT = PAIR_AT + ITEMS
ROWS_AT = SOURCE_AT + OWN + 8
TOTAL_AT = ROWS_AT + OWN + 8
PLAN = TOTAL_AT + 8


PROJECT_VMEM = 54016 * 1024
ATTEND_VMEM = 53760 * 1024


def normalize_input(values, norm_gain):
    center = jnp.mean(values, axis=-1, keepdims=True)
    spread = jnp.mean(jnp.square(values - center), axis=-1, keepdims=True)
    return ((values - center) * lax.rsqrt(spread + EPS) * norm_gain).astype(jnp.bfloat16)


def silu(values):
    half = 0.5 * values
    return half + half * jnp.tanh(half)


def shift(value, axis, steps):
    count = lax.axis_size(axis)
    return lax.ppermute(value, axis, [(i, (i + steps) % count) for i in range(count)])


def project_kernel(near_rows, far_rows, gain_hbm, weight_hbm, near_ref, far_ref, gain, weight, sem):
    copies = [
        pltpu.make_async_copy(gain_hbm, gain, sem.at[0]),
        pltpu.make_async_copy(weight_hbm.at[:, pl.ds(0, D)], weight, sem.at[1]),
    ]
    for copy in copies:
        copy.start()
    rows = jnp.concatenate([near_rows[...], far_rows[...]], axis=0).astype(jnp.float32)
    copies[0].wait()
    normed = normalize_input(rows, gain[...])
    copies[1].wait()
    projected = jnp.dot(normed, weight[...], preferred_element_type=jnp.float32)
    queries = silu(projected).astype(jnp.bfloat16) * jnp.bfloat16(HALF_SCALE)
    near_ref[...] = queries[:BLK]
    far_ref[...] = queries[BLK:]


def project(near, far, norm_gain, qu_weight):
    vmem = pl.BlockSpec(memory_space=pltpu.VMEM)
    hbm = pl.BlockSpec(memory_space=pltpu.HBM)
    return pl.pallas_call(
        project_kernel,
        in_specs=[vmem] * 2 + [hbm] * 2,
        out_specs=[vmem] * 2,
        scratch_shapes=[
            pltpu.VMEM((1, D), jnp.float32),
            pltpu.VMEM((D, D), jnp.bfloat16),
            pltpu.SemaphoreType.DMA((2,)),
        ],
        out_shape=[jax.ShapeDtypeStruct((BLK, D), jnp.bfloat16)] * 2,
        compiler_params=pltpu.CompilerParams(vmem_limit_bytes=PROJECT_VMEM),
        name="project",
    )(near, far, norm_gain.reshape(1, D), qu_weight)


def output_rows():
    return pl.ds(pl.multiple_of((lax.axis_index("zl") * 4 + lax.axis_index("y")) * 16, 16), 16)


def gate_kernel(cand_ref, gain_ref, weight_ref, gate_ref):
    rows = cand_ref[output_rows(), :].astype(jnp.float32)
    normed = normalize_input(rows, gain_ref[...])
    gate_ref[...] = silu(jnp.dot(normed, weight_ref[:, D:], preferred_element_type=jnp.float32))


def project_gate(candidates, norm_gain, qu_weight):
    vmem = pl.BlockSpec(memory_space=pltpu.VMEM)
    return pl.pallas_call(
        gate_kernel,
        in_specs=[vmem] * 3,
        out_specs=vmem,
        out_shape=jax.ShapeDtypeStruct((16, D), jnp.float32),
        compiler_params=pltpu.CompilerParams(vmem_limit_bytes=16 * 1024 * 1024),
        name="gate",
    )(candidates, norm_gain.reshape(1, D), qu_weight)


def finish_kernel(parts_ref, gate_ref, cand_ref, weight_ref, out_ref):
    summed = jnp.sum(parts_ref[...].astype(jnp.float32), axis=0)
    core = lax.axis_index("c")
    gate = jnp.where(core == 0, gate_ref[:8], gate_ref[8:])
    rows = cand_ref[output_rows(), :].astype(jnp.float32)
    rows = jnp.where(core == 0, rows[:8], rows[8:])
    heads = []
    for h in range(H):
        one = summed[:, h * DH : (h + 1) * DH]
        center = jnp.mean(one, axis=-1, keepdims=True)
        spread = jnp.mean(jnp.square(one - center), axis=-1, keepdims=True)
        heads.append((one - center) * lax.rsqrt(spread + EPS))
    mixed = (jnp.concatenate(heads, axis=1) * gate).astype(jnp.bfloat16)
    output = rows + jnp.dot(mixed, weight_ref[...], preferred_element_type=jnp.float32)
    out_ref[...] = output.astype(jnp.bfloat16)


def finish(parts, gate, candidates, out_weight):
    vmem = pl.BlockSpec(memory_space=pltpu.VMEM)
    return pl.pallas_call(
        finish_kernel,
        in_specs=[vmem] * 4,
        out_specs=vmem,
        out_shape=jax.ShapeDtypeStruct((8, D), jnp.bfloat16),
        compiler_params=pltpu.CompilerParams(vmem_limit_bytes=16 * 1024 * 1024),
        name="finish",
    )(parts, gate, candidates, out_weight)


def fetch_used(asked, work, used, own_ref, oth_ref, kvs, sem):
    for s in range(SLOTS + 1):
        used[s] = 0
    for k in range(32):
        for other in range(2):
            value = asked[k, 0, other]
            used[jnp.where(value > 0, 2 * value - 2 + other, SLOTS)] = 1

    def start(s, place):
        for other, ref in enumerate((own_ref, oth_ref)):
            work[SOURCE_AT + place] = 2 * s + other

            @pl.when(used[2 * s + other] > 0)
            def _(place=place, ref=ref):
                pltpu.make_async_copy(ref.at[s], kvs.at[place], sem.at[place]).start()

            place = place + used[2 * s + other]
        return place

    return lax.fori_loop(0, OWN, start, jnp.int32(0))


def list_items(mask, lens, first, count, work):
    core, zh = lax.axis_index("c"), lax.axis_index("zh")
    columns = [first + core * OWN, first + (1 - core) * OWN]
    rows = [(jnp.bitwise_xor(zh, i // 4) * 4 + i % 4) * 2 + core for i in range(8)]

    def block(n, counts):
        s = work[SOURCE_AT + n]
        column = jnp.where(s % 2 == 0, columns[0], columns[1]) + s // 2
        work[ROWS_AT + n] = lens[0, column]
        after = []
        for i in range(8):
            work[i * LIST + counts[i]] = n
            after.append(counts[i] + mask[rows[i], column])
        return tuple(after)

    counts = lax.fori_loop(0, count, block, (jnp.int32(0),) * 8)
    for i in range(8):
        work[i * LIST + counts[i]] = OWN
        work[i * LIST + OWN] = OWN
        work[i * LIST + OWN + 1] = OWN

    pairs = [(counts[i] + 1) // 2 for i in range(8)]
    most = functools.reduce(jnp.maximum, pairs)

    def level(p, n):
        for i in range(8):
            work[BLOCK_AT + n] = i
            work[PAIR_AT + n] = p
            n = n + (pairs[i] > p).astype(jnp.int32)
        return n

    total = lax.fori_loop(0, most, level, jnp.int32(0))
    for k in range(3 * AT_ONCE):
        work[BLOCK_AT + total + k] = 7
        work[PAIR_AT + total + k] = OWN // 2
    return total


def attend_kernel(asked, mask_hbm, lens_hbm, *rest):
    *q_refs, own_ref, oth_ref, out_ref, kvs, q_all, acc, held, sem, work, used, mask, lens, known_sem = rest
    chip = ((lax.axis_index("zh") * 4 + lax.axis_index("x")) * 4 + lax.axis_index("zl")) * 4 + lax.axis_index("y")
    aligned = pl.multiple_of(chip // 2 * 128, 128)
    known = [
        pltpu.make_async_copy(mask_hbm.at[:, pl.ds(aligned, 128)], mask, known_sem.at[0]),
        pltpu.make_async_copy(lens_hbm.at[pl.ds(chip // 2, 1), :], lens, known_sem.at[1]),
    ]
    for copy in known:
        copy.start()
    count = fetch_used(asked, work, used, own_ref, oth_ref, kvs, sem)
    for copy in known:
        copy.wait()
    total = list_items(mask, lens, chip % 2 * SLOTS, count, work)
    kvs[OWN] = jnp.zeros((BLK, 2 * D), jnp.bfloat16)
    acc[...] = jnp.zeros_like(acc)
    for k, ref in enumerate(q_refs):
        q_all[k] = ref[...]

    def arrive(k, _):
        pltpu.make_async_copy(own_ref.at[0], kvs.at[k], sem.at[k]).wait()

        @pl.when(work[ROWS_AT + k] < BLK)
        def _():
            row = lax.broadcasted_iota(jnp.int32, (BLK, D), 0)
            values = kvs[k, :, D:].astype(jnp.float32)
            kvs[k, :, D:] = jnp.where(row < work[ROWS_AT + k], values, 0.0).astype(jnp.bfloat16)

        return 0

    def ensure(n, arrived):
        upto = arrived
        for u in range(AT_ONCE):
            i = work[BLOCK_AT + n * AT_ONCE + u]
            p = work[PAIR_AT + n * AT_ONCE + u]
            for part in range(2):
                block = work[i * LIST + 2 * p + part]
                upto = jnp.maximum(upto, jnp.where(block < OWN, block + 1, 0))
        lax.fori_loop(arrived, upto, arrive, 0)
        return upto

    head = lax.broadcasted_iota(jnp.int32, (BLK, 256), 1) // DH
    my_x = lax.axis_index("x")

    def weights(t, g):
        i = work[BLOCK_AT + t]
        p = work[PAIR_AT + t]
        a = work[i * LIST + 2 * p]
        b = work[i * LIST + 2 * p + 1]
        slot = i // 4 * 4 + lax.rem(my_x - i % 4 + 4, 4)
        cols = slice(g * 256, (g + 1) * 256)
        keys = jnp.concatenate([kvs[a, :, cols], kvs[b, :, cols]], axis=0)
        queries = q_all[slot, :, cols]
        spread = jnp.concatenate([jnp.where(head == h, queries, jnp.zeros_like(queries)) for h in range(4)], axis=0)
        score = lax.dot_general(spread, keys, LAST_DIMS, preferred_element_type=jnp.float32)
        return (score + score * jnp.tanh(score)).astype(jnp.bfloat16)

    def attended(t, g, weight):
        i = work[BLOCK_AT + t]
        p = work[PAIR_AT + t]
        a = work[i * LIST + 2 * p]
        b = work[i * LIST + 2 * p + 1]
        cols = slice(D + g * 256, D + (g + 1) * 256)
        values = jnp.concatenate([kvs[a, :, cols], kvs[b, :, cols]], axis=0)
        every = jnp.dot(weight, values, preferred_element_type=jnp.float32)
        mine = every[:BLK]
        for h in range(1, 4):
            mine = jnp.where(head == h, every[h * BLK : (h + 1) * BLK], mine)
        return mine

    def fill(n, slot):
        for u in range(AT_ONCE):
            for g in range(2):
                held[slot, u, g] = weights(n * AT_ONCE + u, g)

    arrived = ensure(0, jnp.int32(0))
    fill(0, 0)

    def step(n, arrived):
        now = n % 2
        arrived = ensure(n + 1, arrived)
        sums = [attended(n * AT_ONCE + u, g, held[now, u, g]) for u in range(AT_ONCE) for g in range(2)]
        fill(n + 1, 1 - now)
        for u in range(AT_ONCE):
            i = work[BLOCK_AT + n * AT_ONCE + u]
            for g in range(2):
                acc[i, :, g * 256 : (g + 1) * 256] += sums[2 * u + g]
        return arrived

    arrived = lax.fori_loop(0, (total + AT_ONCE - 1) // AT_ONCE, step, arrived)
    lax.fori_loop(arrived, count, arrive, 0)
    for i in range(8):
        for z in range(2):
            for y in range(4):
                first = z * 64 + y * 16
                out_ref[i % 4 * 4 + y, i // 4 * 2 + z] = acc[i, first : first + 16, :].astype(jnp.bfloat16)


def attend(scalars, queries, own, oth):
    smem = pl.BlockSpec(memory_space=pltpu.SMEM)
    vmem = pl.BlockSpec(memory_space=pltpu.VMEM)
    hbm = pl.BlockSpec(memory_space=pltpu.HBM)
    return pl.pallas_call(
        attend_kernel,
        in_specs=[smem] + [hbm] * 2 + [vmem] * 8 + [hbm] * 2,
        out_specs=vmem,
        scratch_shapes=[
            pltpu.VMEM((OWN + 1, BLK, 2 * D), jnp.bfloat16),
            pltpu.VMEM((8, BLK, D), jnp.bfloat16),
            pltpu.VMEM((8, BLK, D), jnp.float32),
            pltpu.VMEM((2, AT_ONCE, 2, 4 * BLK, 256), jnp.bfloat16),
            pltpu.SemaphoreType.DMA((OWN,)),
            pltpu.SMEM((PLAN,), jnp.int32),
            pltpu.SMEM((SLOTS + 8,), jnp.int32),
            pltpu.SMEM((16, 128), jnp.int32),
            pltpu.SMEM((1, 128), jnp.int32),
            pltpu.SemaphoreType.DMA((2,)),
        ],
        out_shape=jax.ShapeDtypeStruct((16, 4, 16, D), jnp.bfloat16),
        compiler_params=pltpu.CompilerParams(vmem_limit_bytes=ATTEND_VMEM),
        cost_estimate=pl.CostEstimate(flops=20_000_000_000, bytes_accessed=8_000_000, transcendentals=0),
        name="attend",
    )(*scalars, *queries, own, oth)


def place_sums_kernel(parts_ref, out_ref):
    core, zh = lax.axis_index("c"), lax.axis_index("zh")
    sums = jnp.sum(parts_ref[...].astype(jnp.float32), axis=0)
    near, far = sums[:32], sums[32:]
    halves = [jnp.where(zh == 0, near, far), jnp.where(zh == 0, far, near)]
    for z in range(2):
        for parity in range(2):
            mine = jnp.where(core == parity, halves[z], 0.0).astype(jnp.bfloat16)
            for k in range(4):
                out_ref[z * 8 + parity * 4 + k] = mine[k * 8 : (k + 1) * 8]


def place_sums(parts):
    vmem = pl.BlockSpec(memory_space=pltpu.VMEM)
    return pl.pallas_call(
        place_sums_kernel,
        in_specs=[vmem],
        out_specs=vmem,
        out_shape=jax.ShapeDtypeStruct((16, 8, D), jnp.bfloat16),
        compiler_params=pltpu.CompilerParams(vmem_limit_bytes=16 * 1024 * 1024),
        name="place_sums",
    )(parts)


def on_device(candidates, norm_gain, qu_weight, out_weight, kv_cache, requests, block_mask, hist_len):
    wanted = requests[0]
    asker = jnp.bitwise_xor(jnp.arange(32)[:, None, None, None], jnp.arange(128)[None, None, :, None])
    to_holder = jnp.sum(jnp.where(wanted // OWN % 32 == asker, wanted % OWN + 1, 0), axis=3)
    asked = lax.all_to_all(to_holder, HIST, 0, 0, tiled=True)

    rows = lax.dynamic_slice_in_dim(candidates, lax.axis_index("c") * BLK, BLK, 0)
    across = shift(rows, "zh", 1)
    across, asked, cache = lax.optimization_barrier((across, asked, kv_cache))
    oth_cache = shift(cache, "c", 1)
    near, far = project(rows, across, norm_gain, qu_weight)
    near_1, far_1, near_3, far_3 = shift(near, "x", 1), shift(far, "x", 1), shift(near, "x", -1), shift(far, "x", -1)
    near_2, far_2 = shift(near_1, "x", 1), shift(far_3, "x", -1)
    queries = (near, near_1, near_2, near_3, far, far_1, far_2, far_3)

    sums = attend((asked, block_mask, hist_len.reshape(-1, 128)), queries, kv_cache, oth_cache)

    parts = lax.all_to_all(sums.reshape(16, 64, D), ("x", "y"), 0, 0, tiled=True)
    parts = lax.all_to_all(place_sums(parts), ("zh", "zl", "c"), 0, 0, tiled=True)
    gate = project_gate(candidates, norm_gain, qu_weight)
    return finish(parts, gate, candidates, out_weight)


def solution(mesh):
    fine = Mesh(mesh.devices.reshape(2, 4, 4, 4, 2), AXES)
    placed = (
        P(CAND, None),
        P(),
        P(),
        P(),
        P(AXES, None, None),
        P(AXES, None),
        P(),
        P(),
    )
    return jax.shard_map(on_device, mesh=fine, in_specs=placed, out_specs=P(AXES, None), check_vma=False)
```

```python
import functools

import jax
import jax.numpy as jnp
from jax import lax
from jax.experimental import pallas as pl
from jax.experimental.pallas import tpu as pltpu
from jax.sharding import Mesh, PartitionSpec as P

H = 8
DH = 64
D = H * DH
BLK = 128
OWN = 32
EPS = 1e-05
HALF_SCALE = 0.0625
LAST_DIMS = (((1,), (1,)), ((), ()))
AXES = ("zh", "x", "zl", "y", "c")
CAND = ("zh", "x")
HIST = ("zl", "y", "c")
SLOTS = 2 * OWN
AT_ONCE = 3
ITEMS = 4 * OWN + 4 * AT_ONCE
LIST = OWN + 4
BLOCK_AT = 8 * LIST
PAIR_AT = BLOCK_AT + ITEMS
SOURCE_AT = PAIR_AT + ITEMS
ROWS_AT = SOURCE_AT + OWN + 8
TOTAL_AT = ROWS_AT + OWN + 8
PLAN = TOTAL_AT + 8


PROJECT_VMEM = 54016 * 1024
ATTEND_VMEM = 53760 * 1024


def normalize_input(values, norm_gain):
    center = jnp.mean(values, axis=-1, keepdims=True)
    spread = jnp.mean(jnp.square(values - center), axis=-1, keepdims=True)
    return ((values - center) * lax.rsqrt(spread + EPS) * norm_gain).astype(jnp.bfloat16)


def silu(values):
    half = 0.5 * values
    return half + half * jnp.tanh(half)


def shift(value, axis, steps):
    count = lax.axis_size(axis)
    return lax.ppermute(value, axis, [(i, (i + steps) % count) for i in range(count)])


def project_kernel(near_rows, far_rows, gain_hbm, weight_hbm, near_ref, far_ref, gain, weight, sem):
    copies = [
        pltpu.make_async_copy(gain_hbm, gain, sem.at[0]),
        pltpu.make_async_copy(weight_hbm.at[:, pl.ds(0, D)], weight, sem.at[1]),
    ]
    for copy in copies:
        copy.start()
    rows = jnp.concatenate([near_rows[...], far_rows[...]], axis=0).astype(jnp.float32)
    copies[0].wait()
    normed = normalize_input(rows, gain[...])
    copies[1].wait()
    projected = jnp.dot(normed, weight[...], preferred_element_type=jnp.float32)
    queries = silu(projected).astype(jnp.bfloat16) * jnp.bfloat16(HALF_SCALE)
    near_ref[...] = queries[:BLK]
    far_ref[...] = queries[BLK:]


def project(near, far, norm_gain, qu_weight):
    vmem = pl.BlockSpec(memory_space=pltpu.VMEM)
    hbm = pl.BlockSpec(memory_space=pltpu.HBM)
    return pl.pallas_call(
        project_kernel,
        in_specs=[vmem] * 2 + [hbm] * 2,
        out_specs=[vmem] * 2,
        scratch_shapes=[
            pltpu.VMEM((1, D), jnp.float32),
            pltpu.VMEM((D, D), jnp.bfloat16),
            pltpu.SemaphoreType.DMA((2,)),
        ],
        out_shape=[jax.ShapeDtypeStruct((BLK, D), jnp.bfloat16)] * 2,
        compiler_params=pltpu.CompilerParams(vmem_limit_bytes=PROJECT_VMEM),
        name="project",
    )(near, far, norm_gain.reshape(1, D), qu_weight)


def output_rows():
    return pl.ds(pl.multiple_of((lax.axis_index("zl") * 4 + lax.axis_index("y")) * 16, 16), 16)


def gate_kernel(cand_ref, gain_ref, weight_ref, gate_ref):
    rows = cand_ref[output_rows(), :].astype(jnp.float32)
    normed = normalize_input(rows, gain_ref[...])
    gate_ref[...] = silu(jnp.dot(normed, weight_ref[:, D:], preferred_element_type=jnp.float32))


def project_gate(candidates, norm_gain, qu_weight):
    vmem = pl.BlockSpec(memory_space=pltpu.VMEM)
    return pl.pallas_call(
        gate_kernel,
        in_specs=[vmem] * 3,
        out_specs=vmem,
        out_shape=jax.ShapeDtypeStruct((16, D), jnp.float32),
        compiler_params=pltpu.CompilerParams(vmem_limit_bytes=16 * 1024 * 1024),
        name="gate",
    )(candidates, norm_gain.reshape(1, D), qu_weight)


def finish_kernel(parts_ref, gate_ref, cand_ref, weight_ref, out_ref):
    summed = jnp.sum(parts_ref[...].astype(jnp.float32), axis=0)
    core = lax.axis_index("c")
    gate = jnp.where(core == 0, gate_ref[:8], gate_ref[8:])
    rows = cand_ref[output_rows(), :].astype(jnp.float32)
    rows = jnp.where(core == 0, rows[:8], rows[8:])
    heads = []
    for h in range(H):
        one = summed[:, h * DH : (h + 1) * DH]
        center = jnp.mean(one, axis=-1, keepdims=True)
        spread = jnp.mean(jnp.square(one - center), axis=-1, keepdims=True)
        heads.append((one - center) * lax.rsqrt(spread + EPS))
    mixed = (jnp.concatenate(heads, axis=1) * gate).astype(jnp.bfloat16)
    output = rows + jnp.dot(mixed, weight_ref[...], preferred_element_type=jnp.float32)
    out_ref[...] = output.astype(jnp.bfloat16)


def finish(parts, gate, candidates, out_weight):
    vmem = pl.BlockSpec(memory_space=pltpu.VMEM)
    return pl.pallas_call(
        finish_kernel,
        in_specs=[vmem] * 4,
        out_specs=vmem,
        out_shape=jax.ShapeDtypeStruct((8, D), jnp.bfloat16),
        compiler_params=pltpu.CompilerParams(vmem_limit_bytes=16 * 1024 * 1024),
        name="finish",
    )(parts, gate, candidates, out_weight)


def mark_used(asked, work, used):
    for s in range(SLOTS + 1):
        used[s] = 0
    for k in range(32):
        for other in range(2):
            value = asked[k, 0, other]
            used[jnp.where(value > 0, 2 * value - 2 + other, SLOTS)] = 1
    place = jnp.int32(0)
    for s in range(SLOTS):
        work[SOURCE_AT + place] = s
        place = place + used[s]
    return place


def list_items(mask, lens, first, count, work):
    core, zh = lax.axis_index("c"), lax.axis_index("zh")
    columns = [first + core * OWN, first + (1 - core) * OWN]
    rows = [(jnp.bitwise_xor(zh, i // 4) * 4 + i % 4) * 2 + core for i in range(8)]

    def block(n, counts):
        s = work[SOURCE_AT + n]
        column = jnp.where(s % 2 == 0, columns[0], columns[1]) + s // 2
        work[ROWS_AT + n] = lens[0, column]
        after = []
        for i in range(8):
            work[i * LIST + counts[i]] = n
            after.append(counts[i] + mask[rows[i], column])
        return tuple(after)

    counts = lax.fori_loop(0, count, block, (jnp.int32(0),) * 8)
    for i in range(8):
        work[i * LIST + counts[i]] = OWN
        work[i * LIST + OWN] = OWN
        work[i * LIST + OWN + 1] = OWN

    pairs = [(counts[i] + 1) // 2 for i in range(8)]
    most = functools.reduce(jnp.maximum, pairs)

    def level(p, n):
        for i in range(8):
            work[BLOCK_AT + n] = i
            work[PAIR_AT + n] = p
            n = n + (pairs[i] > p).astype(jnp.int32)
        return n

    total = lax.fori_loop(0, most, level, jnp.int32(0))
    for k in range(3 * AT_ONCE):
        work[BLOCK_AT + total + k] = 7
        work[PAIR_AT + total + k] = OWN // 2
    return total


def plan_kernel(asked, mask_hbm, lens_hbm, work, used, mask, lens, sem):
    chip = ((lax.axis_index("zh") * 4 + lax.axis_index("x")) * 4 + lax.axis_index("zl")) * 4 + lax.axis_index("y")
    aligned = pl.multiple_of(chip // 2 * 128, 128)
    known = [
        pltpu.make_async_copy(mask_hbm.at[:, pl.ds(aligned, 128)], mask, sem.at[0]),
        pltpu.make_async_copy(lens_hbm.at[pl.ds(chip // 2, 1), :], lens, sem.at[1]),
    ]
    for copy in known:
        copy.start()
    count = mark_used(asked, work, used)
    for copy in known:
        copy.wait()
    work[TOTAL_AT] = list_items(mask, lens, chip % 2 * SLOTS, count, work)
    work[TOTAL_AT + 1] = count


def plan(asked, block_mask, hist_len):
    smem = pl.BlockSpec(memory_space=pltpu.SMEM)
    hbm = pl.BlockSpec(memory_space=pltpu.HBM)
    return pl.pallas_call(
        plan_kernel,
        in_specs=[smem, hbm, hbm],
        out_specs=smem,
        scratch_shapes=[
            pltpu.SMEM((SLOTS + 8,), jnp.int32),
            pltpu.SMEM((16, 128), jnp.int32),
            pltpu.SMEM((1, 128), jnp.int32),
            pltpu.SemaphoreType.DMA((2,)),
        ],
        out_shape=jax.ShapeDtypeStruct((PLAN,), jnp.int32),
        compiler_params=pltpu.CompilerParams(vmem_limit_bytes=ATTEND_VMEM),
        name="plan",
    )(asked, block_mask, hist_len.reshape(-1, 128))


def attend_kernel(work, *rest):
    *q_refs, own_ref, oth_ref, out_ref, kvs, q_all, acc, held, sem = rest
    total, count = work[TOTAL_AT], work[TOTAL_AT + 1]

    def start(k, _):
        s = work[SOURCE_AT + k]

        @pl.when(s % 2 == 0)
        def _():
            pltpu.make_async_copy(own_ref.at[s >> 1], kvs.at[k], sem.at[k]).start()

        @pl.when(s % 2 == 1)
        def _():
            pltpu.make_async_copy(oth_ref.at[s >> 1], kvs.at[k], sem.at[k]).start()

        return 0

    lax.fori_loop(0, count, start, 0)
    kvs[OWN] = jnp.zeros((BLK, 2 * D), jnp.bfloat16)
    acc[...] = jnp.zeros_like(acc)
    for k, ref in enumerate(q_refs):
        q_all[k] = ref[...]

    def arrive(k, _):
        pltpu.make_async_copy(own_ref.at[0], kvs.at[k], sem.at[k]).wait()

        @pl.when(work[ROWS_AT + k] < BLK)
        def _():
            row = lax.broadcasted_iota(jnp.int32, (BLK, D), 0)
            values = kvs[k, :, D:].astype(jnp.float32)
            kvs[k, :, D:] = jnp.where(row < work[ROWS_AT + k], values, 0.0).astype(jnp.bfloat16)

        return 0

    def ensure(n, arrived):
        upto = arrived
        for u in range(AT_ONCE):
            i = work[BLOCK_AT + n * AT_ONCE + u]
            p = work[PAIR_AT + n * AT_ONCE + u]
            for part in range(2):
                block = work[i * LIST + 2 * p + part]
                upto = jnp.maximum(upto, jnp.where(block < OWN, block + 1, 0))
        lax.fori_loop(arrived, upto, arrive, 0)
        return upto

    head = lax.broadcasted_iota(jnp.int32, (BLK, 256), 1) // DH
    my_x = lax.axis_index("x")

    def weights(t, g):
        i = work[BLOCK_AT + t]
        p = work[PAIR_AT + t]
        a = work[i * LIST + 2 * p]
        b = work[i * LIST + 2 * p + 1]
        slot = i // 4 * 4 + lax.rem(my_x - i % 4 + 4, 4)
        cols = slice(g * 256, (g + 1) * 256)
        keys = jnp.concatenate([kvs[a, :, cols], kvs[b, :, cols]], axis=0)
        queries = q_all[slot, :, cols]
        spread = jnp.concatenate([jnp.where(head == h, queries, jnp.zeros_like(queries)) for h in range(4)], axis=0)
        score = lax.dot_general(spread, keys, LAST_DIMS, preferred_element_type=jnp.float32)
        return (score + score * jnp.tanh(score)).astype(jnp.bfloat16)

    def attended(t, g, weight):
        i = work[BLOCK_AT + t]
        p = work[PAIR_AT + t]
        a = work[i * LIST + 2 * p]
        b = work[i * LIST + 2 * p + 1]
        cols = slice(D + g * 256, D + (g + 1) * 256)
        values = jnp.concatenate([kvs[a, :, cols], kvs[b, :, cols]], axis=0)
        every = jnp.dot(weight, values, preferred_element_type=jnp.float32)
        mine = every[:BLK]
        for h in range(1, 4):
            mine = jnp.where(head == h, every[h * BLK : (h + 1) * BLK], mine)
        return mine

    def fill(n, slot):
        for u in range(AT_ONCE):
            for g in range(2):
                held[slot, u, g] = weights(n * AT_ONCE + u, g)

    arrived = ensure(0, jnp.int32(0))
    fill(0, 0)

    def step(n, arrived):
        now = n % 2
        arrived = ensure(n + 1, arrived)
        sums = [attended(n * AT_ONCE + u, g, held[now, u, g]) for u in range(AT_ONCE) for g in range(2)]
        fill(n + 1, 1 - now)
        for u in range(AT_ONCE):
            i = work[BLOCK_AT + n * AT_ONCE + u]
            for g in range(2):
                acc[i, :, g * 256 : (g + 1) * 256] += sums[2 * u + g]
        return arrived

    arrived = lax.fori_loop(0, (total + AT_ONCE - 1) // AT_ONCE, step, arrived)
    lax.fori_loop(arrived, count, arrive, 0)
    for i in range(8):
        for z in range(2):
            for y in range(4):
                first = z * 64 + y * 16
                out_ref[i % 4 * 4 + y, i // 4 * 2 + z] = acc[i, first : first + 16, :].astype(jnp.bfloat16)


def attend(work, queries, own, oth):
    smem = pl.BlockSpec(memory_space=pltpu.SMEM)
    vmem = pl.BlockSpec(memory_space=pltpu.VMEM)
    hbm = pl.BlockSpec(memory_space=pltpu.HBM)
    return pl.pallas_call(
        attend_kernel,
        in_specs=[smem] + [vmem] * 8 + [hbm] * 2,
        out_specs=vmem,
        scratch_shapes=[
            pltpu.VMEM((OWN + 1, BLK, 2 * D), jnp.bfloat16),
            pltpu.VMEM((8, BLK, D), jnp.bfloat16),
            pltpu.VMEM((8, BLK, D), jnp.float32),
            pltpu.VMEM((2, AT_ONCE, 2, 4 * BLK, 256), jnp.bfloat16),
            pltpu.SemaphoreType.DMA((OWN,)),
        ],
        out_shape=jax.ShapeDtypeStruct((16, 4, 16, D), jnp.bfloat16),
        compiler_params=pltpu.CompilerParams(vmem_limit_bytes=ATTEND_VMEM),
        cost_estimate=pl.CostEstimate(flops=20_000_000_000, bytes_accessed=8_000_000, transcendentals=0),
        name="attend",
    )(work, *queries, own, oth)


def place_sums_kernel(parts_ref, out_ref):
    core, zh = lax.axis_index("c"), lax.axis_index("zh")
    sums = jnp.sum(parts_ref[...].astype(jnp.float32), axis=0)
    near, far = sums[:32], sums[32:]
    halves = [jnp.where(zh == 0, near, far), jnp.where(zh == 0, far, near)]
    for z in range(2):
        for parity in range(2):
            mine = jnp.where(core == parity, halves[z], 0.0).astype(jnp.bfloat16)
            for k in range(4):
                out_ref[z * 8 + parity * 4 + k] = mine[k * 8 : (k + 1) * 8]


def place_sums(parts):
    vmem = pl.BlockSpec(memory_space=pltpu.VMEM)
    return pl.pallas_call(
        place_sums_kernel,
        in_specs=[vmem],
        out_specs=vmem,
        out_shape=jax.ShapeDtypeStruct((16, 8, D), jnp.bfloat16),
        compiler_params=pltpu.CompilerParams(vmem_limit_bytes=16 * 1024 * 1024),
        name="place_sums",
    )(parts)


def on_device(candidates, norm_gain, qu_weight, out_weight, kv_cache, requests, block_mask, hist_len):
    oth_cache = shift(kv_cache, "c", 1)

    wanted = requests[0]
    asker = jnp.bitwise_xor(jnp.arange(32)[:, None, None, None], jnp.arange(128)[None, None, :, None])
    to_holder = jnp.sum(jnp.where(wanted // OWN % 32 == asker, wanted % OWN + 1, 0), axis=3)
    asked = lax.all_to_all(to_holder, HIST, 0, 0, tiled=True)

    rows = lax.dynamic_slice_in_dim(candidates, lax.axis_index("c") * BLK, BLK, 0)
    across = shift(rows, "zh", 1)
    across, asked = lax.optimization_barrier((across, asked))
    near, far = project(rows, across, norm_gain, qu_weight)
    near_1, far_1, near_3, far_3 = shift(near, "x", 1), shift(far, "x", 1), shift(near, "x", -1), shift(far, "x", -1)
    near_2, far_2 = shift(near_1, "x", 1), shift(far_3, "x", -1)
    queries = (near, near_1, near_2, near_3, far, far_1, far_2, far_3)

    sums = attend(plan(asked, block_mask, hist_len), queries, kv_cache, oth_cache)

    parts = lax.all_to_all(sums.reshape(16, 64, D), ("x", "y"), 0, 0, tiled=True)
    parts = lax.all_to_all(place_sums(parts), ("zh", "zl", "c"), 0, 0, tiled=True)
    gate = project_gate(candidates, norm_gain, qu_weight)
    return finish(parts, gate, candidates, out_weight)


def solution(mesh):
    fine = Mesh(mesh.devices.reshape(2, 4, 4, 4, 2), AXES)
    placed = (
        P(CAND, None),
        P(),
        P(),
        P(),
        P(AXES, None, None),
        P(AXES, None),
        P(),
        P(),
    )
    return jax.shard_map(on_device, mesh=fine, in_specs=placed, out_specs=P(AXES, None), check_vma=False)
```

```python
import functools

import jax
import jax.numpy as jnp
from jax import lax
from jax.experimental import pallas as pl
from jax.experimental.pallas import tpu as pltpu
from jax.sharding import Mesh, PartitionSpec as P

H = 8
DH = 64
D = H * DH
BLK = 128
OWN = 32
EPS = 1e-05
HALF_SCALE = 0.0625
LAST_DIMS = (((1,), (1,)), ((), ()))
AXES = ("zh", "x", "zl", "y", "c")
CAND = ("zh", "x")
HIST = ("zl", "y", "c")
SLOTS = 2 * OWN
AT_ONCE = 3
ITEMS = 4 * OWN + 4 * AT_ONCE
LIST = OWN + 4
BLOCK_AT = 8 * LIST
PAIR_AT = BLOCK_AT + ITEMS
SOURCE_AT = PAIR_AT + ITEMS
ROWS_AT = SOURCE_AT + OWN + 8
TOTAL_AT = ROWS_AT + OWN + 8
PLAN = TOTAL_AT + 8


PROJECT_VMEM = 54016 * 1024
ATTEND_VMEM = 53760 * 1024


def normalize_input(values, norm_gain):
    center = jnp.mean(values, axis=-1, keepdims=True)
    spread = jnp.mean(jnp.square(values - center), axis=-1, keepdims=True)
    return ((values - center) * lax.rsqrt(spread + EPS) * norm_gain).astype(jnp.bfloat16)


def silu(values):
    half = 0.5 * values
    return half + half * jnp.tanh(half)


def shift(value, axis, steps):
    count = lax.axis_size(axis)
    return lax.ppermute(value, axis, [(i, (i + steps) % count) for i in range(count)])


def project_kernel(near_rows, far_rows, gain_hbm, weight_hbm, near_ref, far_ref, gain, weight, sem):
    copies = [
        pltpu.make_async_copy(gain_hbm, gain, sem.at[0]),
        pltpu.make_async_copy(weight_hbm.at[:, pl.ds(0, D)], weight, sem.at[1]),
    ]
    for copy in copies:
        copy.start()
    rows = jnp.concatenate([near_rows[...], far_rows[...]], axis=0).astype(jnp.float32)
    copies[0].wait()
    normed = normalize_input(rows, gain[...])
    copies[1].wait()
    projected = jnp.dot(normed, weight[...], preferred_element_type=jnp.float32)
    queries = silu(projected).astype(jnp.bfloat16) * jnp.bfloat16(HALF_SCALE)
    near_ref[...] = queries[:BLK]
    far_ref[...] = queries[BLK:]


def project(near, far, norm_gain, qu_weight):
    vmem = pl.BlockSpec(memory_space=pltpu.VMEM)
    hbm = pl.BlockSpec(memory_space=pltpu.HBM)
    return pl.pallas_call(
        project_kernel,
        in_specs=[vmem] * 2 + [hbm] * 2,
        out_specs=[vmem] * 2,
        scratch_shapes=[
            pltpu.VMEM((1, D), jnp.float32),
            pltpu.VMEM((D, D), jnp.bfloat16),
            pltpu.SemaphoreType.DMA((2,)),
        ],
        out_shape=[jax.ShapeDtypeStruct((BLK, D), jnp.bfloat16)] * 2,
        compiler_params=pltpu.CompilerParams(vmem_limit_bytes=PROJECT_VMEM),
        name="project",
    )(near, far, norm_gain.reshape(1, D), qu_weight)


def output_rows():
    return pl.ds(pl.multiple_of((lax.axis_index("zl") * 4 + lax.axis_index("y")) * 16, 16), 16)


def gate_kernel(cand_ref, gain_ref, weight_ref, gate_ref):
    rows = cand_ref[output_rows(), :].astype(jnp.float32)
    normed = normalize_input(rows, gain_ref[...])
    gate_ref[...] = silu(jnp.dot(normed, weight_ref[:, D:], preferred_element_type=jnp.float32))


def project_gate(candidates, norm_gain, qu_weight):
    vmem = pl.BlockSpec(memory_space=pltpu.VMEM)
    return pl.pallas_call(
        gate_kernel,
        in_specs=[vmem] * 3,
        out_specs=vmem,
        out_shape=jax.ShapeDtypeStruct((16, D), jnp.float32),
        compiler_params=pltpu.CompilerParams(vmem_limit_bytes=16 * 1024 * 1024),
        name="gate",
    )(candidates, norm_gain.reshape(1, D), qu_weight)


def finish_kernel(parts_ref, gate_ref, cand_ref, weight_ref, out_ref):
    summed = jnp.sum(parts_ref[...].astype(jnp.float32), axis=0)
    core = lax.axis_index("c")
    gate = jnp.where(core == 0, gate_ref[:8], gate_ref[8:])
    rows = cand_ref[output_rows(), :].astype(jnp.float32)
    rows = jnp.where(core == 0, rows[:8], rows[8:])
    heads = []
    for h in range(H):
        one = summed[:, h * DH : (h + 1) * DH]
        center = jnp.mean(one, axis=-1, keepdims=True)
        spread = jnp.mean(jnp.square(one - center), axis=-1, keepdims=True)
        heads.append((one - center) * lax.rsqrt(spread + EPS))
    mixed = (jnp.concatenate(heads, axis=1) * gate).astype(jnp.bfloat16)
    output = rows + jnp.dot(mixed, weight_ref[...], preferred_element_type=jnp.float32)
    out_ref[...] = output.astype(jnp.bfloat16)


def finish(parts, gate, candidates, out_weight):
    vmem = pl.BlockSpec(memory_space=pltpu.VMEM)
    return pl.pallas_call(
        finish_kernel,
        in_specs=[vmem] * 4,
        out_specs=vmem,
        out_shape=jax.ShapeDtypeStruct((8, D), jnp.bfloat16),
        compiler_params=pltpu.CompilerParams(vmem_limit_bytes=16 * 1024 * 1024),
        name="finish",
    )(parts, gate, candidates, out_weight)


def mark_used(asked, work, used):
    for s in range(SLOTS + 1):
        used[s] = 0
    for k in range(32):
        for other in range(2):
            value = asked[k, 0, other]
            used[jnp.where(value > 0, 2 * value - 2 + other, SLOTS)] = 1
    place = jnp.int32(0)
    for s in range(SLOTS):
        work[SOURCE_AT + place] = s
        place = place + used[s]
    return place


def list_items(mask, lens, count, work):
    core, zh = lax.axis_index("c"), lax.axis_index("zh")
    columns = [core * OWN, (1 - core) * OWN]
    rows = [(jnp.bitwise_xor(zh, i // 4) * 4 + i % 4) * 2 + core for i in range(8)]

    def block(n, counts):
        s = work[SOURCE_AT + n]
        column = jnp.where((s & 1) == 0, columns[0], columns[1]) + (s >> 1)
        work[ROWS_AT + n] = lens[column]
        after = []
        for i in range(8):
            work[i * LIST + counts[i]] = n
            after.append(counts[i] + mask[rows[i], column])
        return tuple(after)

    counts = lax.fori_loop(0, count, block, (jnp.int32(0),) * 8)
    for i in range(8):
        work[i * LIST + counts[i]] = OWN
        work[i * LIST + OWN] = OWN
        work[i * LIST + OWN + 1] = OWN

    pairs = [(counts[i] + 1) // 2 for i in range(8)]
    most = functools.reduce(jnp.maximum, pairs)

    def level(p, n):
        for i in range(8):
            work[BLOCK_AT + n] = i
            work[PAIR_AT + n] = p
            n = n + (pairs[i] > p).astype(jnp.int32)
        return n

    total = lax.fori_loop(0, most, level, jnp.int32(0))
    for k in range(3 * AT_ONCE):
        work[BLOCK_AT + total + k] = 7
        work[PAIR_AT + total + k] = OWN // 2
    return total


def plan_kernel(asked, mask, lens, work, used):
    count = mark_used(asked, work, used)
    work[TOTAL_AT] = list_items(mask, lens, count, work)
    work[TOTAL_AT + 1] = count


def plan(asked, mask, lens):
    smem = pl.BlockSpec(memory_space=pltpu.SMEM)
    return pl.pallas_call(
        plan_kernel,
        in_specs=[smem] * 3,
        out_specs=smem,
        scratch_shapes=[pltpu.SMEM((SLOTS + 8,), jnp.int32)],
        out_shape=jax.ShapeDtypeStruct((PLAN,), jnp.int32),
        compiler_params=pltpu.CompilerParams(vmem_limit_bytes=4 * 1024 * 1024),
        name="plan",
    )(asked, mask, lens)


def attend_kernel(work, *rest):
    *q_refs, own_ref, oth_ref, out_ref, kvs, q_all, acc, held, sem = rest
    total, count = work[TOTAL_AT], work[TOTAL_AT + 1]

    def start(k, _):
        s = work[SOURCE_AT + k]

        @pl.when(s % 2 == 0)
        def _():
            pltpu.make_async_copy(own_ref.at[s >> 1], kvs.at[k], sem.at[k]).start()

        @pl.when(s % 2 == 1)
        def _():
            pltpu.make_async_copy(oth_ref.at[s >> 1], kvs.at[k], sem.at[k]).start()

        return 0

    lax.fori_loop(0, count, start, 0)
    kvs[OWN] = jnp.zeros((BLK, 2 * D), jnp.bfloat16)
    acc[...] = jnp.zeros_like(acc)
    for k, ref in enumerate(q_refs):
        q_all[k] = ref[...]

    def arrive(k, _):
        pltpu.make_async_copy(own_ref.at[0], kvs.at[k], sem.at[k]).wait()

        @pl.when(work[ROWS_AT + k] < BLK)
        def _():
            row = lax.broadcasted_iota(jnp.int32, (BLK, D), 0)
            values = kvs[k, :, D:].astype(jnp.float32)
            kvs[k, :, D:] = jnp.where(row < work[ROWS_AT + k], values, 0.0).astype(jnp.bfloat16)

        return 0

    def ensure(n, arrived):
        upto = arrived
        for u in range(AT_ONCE):
            i = work[BLOCK_AT + n * AT_ONCE + u]
            p = work[PAIR_AT + n * AT_ONCE + u]
            for part in range(2):
                block = work[i * LIST + 2 * p + part]
                upto = jnp.maximum(upto, jnp.where(block < OWN, block + 1, 0))
        lax.fori_loop(arrived, upto, arrive, 0)
        return upto

    head = lax.broadcasted_iota(jnp.int32, (BLK, 256), 1) // DH
    my_x = lax.axis_index("x")

    def weights(t, g):
        i = work[BLOCK_AT + t]
        p = work[PAIR_AT + t]
        a = work[i * LIST + 2 * p]
        b = work[i * LIST + 2 * p + 1]
        slot = i // 4 * 4 + lax.rem(my_x - i % 4 + 4, 4)
        cols = slice(g * 256, (g + 1) * 256)
        keys = jnp.concatenate([kvs[a, :, cols], kvs[b, :, cols]], axis=0)
        queries = q_all[slot, :, cols]
        spread = jnp.concatenate([jnp.where(head == h, queries, jnp.zeros_like(queries)) for h in range(4)], axis=0)
        score = lax.dot_general(spread, keys, LAST_DIMS, preferred_element_type=jnp.float32)
        return (score + score * jnp.tanh(score)).astype(jnp.bfloat16)

    def attended(t, g, weight):
        i = work[BLOCK_AT + t]
        p = work[PAIR_AT + t]
        a = work[i * LIST + 2 * p]
        b = work[i * LIST + 2 * p + 1]
        cols = slice(D + g * 256, D + (g + 1) * 256)
        values = jnp.concatenate([kvs[a, :, cols], kvs[b, :, cols]], axis=0)
        every = jnp.dot(weight, values, preferred_element_type=jnp.float32)
        mine = every[:BLK]
        for h in range(1, 4):
            mine = jnp.where(head == h, every[h * BLK : (h + 1) * BLK], mine)
        return mine

    def fill(n, slot):
        for u in range(AT_ONCE):
            for g in range(2):
                held[slot, u, g] = weights(n * AT_ONCE + u, g)

    arrived = ensure(0, jnp.int32(0))
    fill(0, 0)

    def step(n, arrived):
        now = n % 2
        arrived = ensure(n + 1, arrived)
        sums = [attended(n * AT_ONCE + u, g, held[now, u, g]) for u in range(AT_ONCE) for g in range(2)]
        fill(n + 1, 1 - now)
        for u in range(AT_ONCE):
            i = work[BLOCK_AT + n * AT_ONCE + u]
            for g in range(2):
                acc[i, :, g * 256 : (g + 1) * 256] += sums[2 * u + g]
        return arrived

    arrived = lax.fori_loop(0, (total + AT_ONCE - 1) // AT_ONCE, step, arrived)
    lax.fori_loop(arrived, count, arrive, 0)
    for i in range(8):
        for z in range(2):
            for y in range(4):
                first = z * 64 + y * 16
                out_ref[i % 4 * 4 + y, i // 4 * 2 + z] = acc[i, first : first + 16, :].astype(jnp.bfloat16)


def attend(work, queries, own, oth):
    smem = pl.BlockSpec(memory_space=pltpu.SMEM)
    vmem = pl.BlockSpec(memory_space=pltpu.VMEM)
    hbm = pl.BlockSpec(memory_space=pltpu.HBM)
    return pl.pallas_call(
        attend_kernel,
        in_specs=[smem] + [vmem] * 8 + [hbm] * 2,
        out_specs=vmem,
        scratch_shapes=[
            pltpu.VMEM((OWN + 1, BLK, 2 * D), jnp.bfloat16),
            pltpu.VMEM((8, BLK, D), jnp.bfloat16),
            pltpu.VMEM((8, BLK, D), jnp.float32),
            pltpu.VMEM((2, AT_ONCE, 2, 4 * BLK, 256), jnp.bfloat16),
            pltpu.SemaphoreType.DMA((OWN,)),
        ],
        out_shape=jax.ShapeDtypeStruct((16, 4, 16, D), jnp.bfloat16),
        compiler_params=pltpu.CompilerParams(vmem_limit_bytes=ATTEND_VMEM),
        cost_estimate=pl.CostEstimate(flops=20_000_000_000, bytes_accessed=8_000_000, transcendentals=0),
        name="attend",
    )(work, *queries, own, oth)


def place_sums_kernel(parts_ref, out_ref):
    core, zh = lax.axis_index("c"), lax.axis_index("zh")
    sums = jnp.sum(parts_ref[...].astype(jnp.float32), axis=0)
    near, far = sums[:32], sums[32:]
    halves = [jnp.where(zh == 0, near, far), jnp.where(zh == 0, far, near)]
    for z in range(2):
        for parity in range(2):
            mine = jnp.where(core == parity, halves[z], 0.0).astype(jnp.bfloat16)
            for k in range(4):
                out_ref[z * 8 + parity * 4 + k] = mine[k * 8 : (k + 1) * 8]


def place_sums(parts):
    vmem = pl.BlockSpec(memory_space=pltpu.VMEM)
    return pl.pallas_call(
        place_sums_kernel,
        in_specs=[vmem],
        out_specs=vmem,
        out_shape=jax.ShapeDtypeStruct((16, 8, D), jnp.bfloat16),
        compiler_params=pltpu.CompilerParams(vmem_limit_bytes=16 * 1024 * 1024),
        name="place_sums",
    )(parts)


def on_device(candidates, norm_gain, qu_weight, out_weight, kv_cache, requests, block_mask, hist_len):
    oth_cache = shift(kv_cache, "c", 1)

    wanted = requests[0]
    asker = jnp.bitwise_xor(jnp.arange(32)[:, None, None, None], jnp.arange(128)[None, None, :, None])
    to_holder = jnp.sum(jnp.where(wanted // OWN % 32 == asker, wanted % OWN + 1, 0), axis=3)
    asked = lax.all_to_all(to_holder, HIST, 0, 0, tiled=True)

    rows = lax.dynamic_slice_in_dim(candidates, lax.axis_index("c") * BLK, BLK, 0)
    across = shift(rows, "zh", 1)
    zh, x, zl, y = (lax.axis_index(a) for a in AXES[:4])
    first_slot = (((zh * 4 + x) * 4 + zl) * 4 + y) * SLOTS
    mask = lax.dynamic_slice_in_dim(block_mask, first_slot, SLOTS, 1)
    lens = lax.dynamic_slice_in_dim(hist_len, first_slot, SLOTS, 0)
    across, asked, mask, lens = lax.optimization_barrier((across, asked, mask, lens))
    near, far = project(rows, across, norm_gain, qu_weight)
    near_1, far_1, near_3, far_3 = shift(near, "x", 1), shift(far, "x", 1), shift(near, "x", -1), shift(far, "x", -1)
    near_2, far_2 = shift(near_1, "x", 1), shift(far_3, "x", -1)
    queries = (near, near_1, near_2, near_3, far, far_1, far_2, far_3)

    sums = attend(plan(asked, mask, lens), queries, kv_cache, oth_cache)

    parts = lax.all_to_all(sums.reshape(16, 64, D), ("x", "y"), 0, 0, tiled=True)
    parts = lax.all_to_all(place_sums(parts), ("zh", "zl", "c"), 0, 0, tiled=True)
    gate = project_gate(candidates, norm_gain, qu_weight)
    return finish(parts, gate, candidates, out_weight)


def solution(mesh):
    fine = Mesh(mesh.devices.reshape(2, 4, 4, 4, 2), AXES)
    placed = (
        P(CAND, None),
        P(),
        P(),
        P(),
        P(AXES, None, None),
        P(AXES, None),
        P(),
        P(),
    )
    return jax.shard_map(on_device, mesh=fine, in_specs=placed, out_specs=P(AXES, None), check_vma=False)
```

```python
import functools

import jax
import jax.numpy as jnp
from jax import lax
from jax.experimental import pallas as pl
from jax.experimental.pallas import tpu as pltpu
from jax.sharding import Mesh, PartitionSpec as P

H = 8
DH = 64
D = H * DH
BLK = 128
OWN = 32
EPS = 1e-05
HALF_SCALE = 0.0625
LAST_DIMS = (((1,), (1,)), ((), ()))
AXES = ("zh", "x", "zl", "y", "c")
CAND = ("zh", "x")
HIST = ("zl", "y", "c")
SLOTS = 2 * OWN
AT_ONCE = 4
ITEMS = 4 * OWN + 4 * AT_ONCE
LIST = OWN + 4
BLOCK_AT = 8 * LIST
PAIR_AT = BLOCK_AT + ITEMS
SOURCE_AT = PAIR_AT + ITEMS
ROWS_AT = SOURCE_AT + OWN + 8
TOTAL_AT = ROWS_AT + OWN + 8
PLAN = TOTAL_AT + 8


PROJECT_VMEM = 54016 * 1024
ATTEND_VMEM = 53760 * 1024


def normalize_input(values, norm_gain):
    center = jnp.mean(values, axis=-1, keepdims=True)
    spread = jnp.mean(jnp.square(values - center), axis=-1, keepdims=True)
    return ((values - center) * lax.rsqrt(spread + EPS) * norm_gain).astype(jnp.bfloat16)


def silu(values):
    half = 0.5 * values
    return half + half * jnp.tanh(half)


def shift(value, axis, steps):
    count = lax.axis_size(axis)
    return lax.ppermute(value, axis, [(i, (i + steps) % count) for i in range(count)])


def project_kernel(near_rows, far_rows, gain_hbm, weight_hbm, near_ref, far_ref, gain, weight, sem):
    copies = [
        pltpu.make_async_copy(gain_hbm, gain, sem.at[0]),
        pltpu.make_async_copy(weight_hbm.at[:, pl.ds(0, D)], weight, sem.at[1]),
    ]
    for copy in copies:
        copy.start()
    rows = jnp.concatenate([near_rows[...], far_rows[...]], axis=0).astype(jnp.float32)
    copies[0].wait()
    normed = normalize_input(rows, gain[...])
    copies[1].wait()
    projected = jnp.dot(normed, weight[...], preferred_element_type=jnp.float32)
    queries = silu(projected).astype(jnp.bfloat16) * jnp.bfloat16(HALF_SCALE)
    near_ref[...] = queries[:BLK]
    far_ref[...] = queries[BLK:]


def project(near, far, norm_gain, qu_weight):
    vmem = pl.BlockSpec(memory_space=pltpu.VMEM)
    hbm = pl.BlockSpec(memory_space=pltpu.HBM)
    return pl.pallas_call(
        project_kernel,
        in_specs=[vmem] * 2 + [hbm] * 2,
        out_specs=[vmem] * 2,
        scratch_shapes=[
            pltpu.VMEM((1, D), jnp.float32),
            pltpu.VMEM((D, D), jnp.bfloat16),
            pltpu.SemaphoreType.DMA((2,)),
        ],
        out_shape=[jax.ShapeDtypeStruct((BLK, D), jnp.bfloat16)] * 2,
        compiler_params=pltpu.CompilerParams(vmem_limit_bytes=PROJECT_VMEM),
        name="project",
    )(near, far, norm_gain.reshape(1, D), qu_weight)


def output_rows():
    return pl.ds(pl.multiple_of((lax.axis_index("zl") * 4 + lax.axis_index("y")) * 16, 16), 16)


def gate_kernel(cand_ref, gain_ref, weight_ref, gate_ref):
    rows = cand_ref[output_rows(), :].astype(jnp.float32)
    normed = normalize_input(rows, gain_ref[...])
    gate_ref[...] = silu(jnp.dot(normed, weight_ref[:, D:], preferred_element_type=jnp.float32))


def project_gate(candidates, norm_gain, qu_weight):
    vmem = pl.BlockSpec(memory_space=pltpu.VMEM)
    return pl.pallas_call(
        gate_kernel,
        in_specs=[vmem] * 3,
        out_specs=vmem,
        out_shape=jax.ShapeDtypeStruct((16, D), jnp.float32),
        compiler_params=pltpu.CompilerParams(vmem_limit_bytes=16 * 1024 * 1024),
        name="gate",
    )(candidates, norm_gain.reshape(1, D), qu_weight)


def finish_kernel(parts_ref, gate_ref, cand_ref, weight_ref, out_ref):
    summed = jnp.sum(parts_ref[...].astype(jnp.float32), axis=0)
    core = lax.axis_index("c")
    gate = jnp.where(core == 0, gate_ref[:8], gate_ref[8:])
    rows = cand_ref[output_rows(), :].astype(jnp.float32)
    rows = jnp.where(core == 0, rows[:8], rows[8:])
    heads = []
    for h in range(H):
        one = summed[:, h * DH : (h + 1) * DH]
        center = jnp.mean(one, axis=-1, keepdims=True)
        spread = jnp.mean(jnp.square(one - center), axis=-1, keepdims=True)
        heads.append((one - center) * lax.rsqrt(spread + EPS))
    mixed = (jnp.concatenate(heads, axis=1) * gate).astype(jnp.bfloat16)
    output = rows + jnp.dot(mixed, weight_ref[...], preferred_element_type=jnp.float32)
    out_ref[...] = output.astype(jnp.bfloat16)


def finish(parts, gate, candidates, out_weight):
    vmem = pl.BlockSpec(memory_space=pltpu.VMEM)
    return pl.pallas_call(
        finish_kernel,
        in_specs=[vmem] * 4,
        out_specs=vmem,
        out_shape=jax.ShapeDtypeStruct((8, D), jnp.bfloat16),
        compiler_params=pltpu.CompilerParams(vmem_limit_bytes=16 * 1024 * 1024),
        name="finish",
    )(parts, gate, candidates, out_weight)


def mark_used(asked, work, used):
    for s in range(SLOTS + 1):
        used[s] = 0
    for k in range(32):
        for other in range(2):
            value = asked[k, 0, other]
            used[jnp.where(value > 0, 2 * value - 2 + other, SLOTS)] = 1
    place = jnp.int32(0)
    for s in range(SLOTS):
        work[SOURCE_AT + place] = s
        place = place + used[s]
    return place


def list_items(mask, lens, count, work):
    core, zh = lax.axis_index("c"), lax.axis_index("zh")
    columns = [core * OWN, (1 - core) * OWN]
    rows = [(jnp.bitwise_xor(zh, i // 4) * 4 + i % 4) * 2 + core for i in range(8)]

    def block(n, counts):
        s = work[SOURCE_AT + n]
        column = jnp.where((s & 1) == 0, columns[0], columns[1]) + (s >> 1)
        work[ROWS_AT + n] = lens[column]
        after = []
        for i in range(8):
            work[i * LIST + counts[i]] = n
            after.append(counts[i] + mask[rows[i], column])
        return tuple(after)

    counts = lax.fori_loop(0, count, block, (jnp.int32(0),) * 8)
    for i in range(8):
        work[i * LIST + counts[i]] = OWN
        work[i * LIST + OWN] = OWN
        work[i * LIST + OWN + 1] = OWN

    pairs = [(counts[i] + 1) // 2 for i in range(8)]
    most = functools.reduce(jnp.maximum, pairs)

    def level(p, n):
        for i in range(8):
            work[BLOCK_AT + n] = i
            work[PAIR_AT + n] = p
            n = n + (pairs[i] > p).astype(jnp.int32)
        return n

    total = lax.fori_loop(0, most, level, jnp.int32(0))
    for k in range(3 * AT_ONCE):
        work[BLOCK_AT + total + k] = 7
        work[PAIR_AT + total + k] = OWN // 2
    return total


def plan_kernel(asked, mask, lens, work, used):
    count = mark_used(asked, work, used)
    work[TOTAL_AT] = list_items(mask, lens, count, work)
    work[TOTAL_AT + 1] = count


def plan(asked, mask, lens):
    smem = pl.BlockSpec(memory_space=pltpu.SMEM)
    return pl.pallas_call(
        plan_kernel,
        in_specs=[smem] * 3,
        out_specs=smem,
        scratch_shapes=[pltpu.SMEM((SLOTS + 8,), jnp.int32)],
        out_shape=jax.ShapeDtypeStruct((PLAN,), jnp.int32),
        compiler_params=pltpu.CompilerParams(vmem_limit_bytes=4 * 1024 * 1024),
        name="plan",
    )(asked, mask, lens)


def attend_kernel(work, *rest):
    *q_refs, own_ref, oth_ref, out_ref, kvs, q_all, acc, held, sem = rest
    total, count = work[TOTAL_AT], work[TOTAL_AT + 1]

    def start(k, _):
        s = work[SOURCE_AT + k]

        @pl.when(s % 2 == 0)
        def _():
            pltpu.make_async_copy(own_ref.at[s >> 1], kvs.at[k], sem.at[k]).start()

        @pl.when(s % 2 == 1)
        def _():
            pltpu.make_async_copy(oth_ref.at[s >> 1], kvs.at[k], sem.at[k]).start()

        return 0

    lax.fori_loop(0, count, start, 0)
    kvs[OWN] = jnp.zeros((BLK, 2 * D), jnp.bfloat16)
    acc[...] = jnp.zeros_like(acc)
    for k, ref in enumerate(q_refs):
        q_all[k] = ref[...]

    def arrive(k, _):
        pltpu.make_async_copy(own_ref.at[0], kvs.at[k], sem.at[k]).wait()

        @pl.when(work[ROWS_AT + k] < BLK)
        def _():
            row = lax.broadcasted_iota(jnp.int32, (BLK, D), 0)
            values = kvs[k, :, D:].astype(jnp.float32)
            kvs[k, :, D:] = jnp.where(row < work[ROWS_AT + k], values, 0.0).astype(jnp.bfloat16)

        return 0

    def ensure(n, arrived):
        upto = arrived
        for u in range(AT_ONCE):
            i = work[BLOCK_AT + n * AT_ONCE + u]
            p = work[PAIR_AT + n * AT_ONCE + u]
            for part in range(2):
                block = work[i * LIST + 2 * p + part]
                upto = jnp.maximum(upto, jnp.where(block < OWN, block + 1, 0))
        lax.fori_loop(arrived, upto, arrive, 0)
        return upto

    head = lax.broadcasted_iota(jnp.int32, (BLK, 256), 1) // DH
    my_x = lax.axis_index("x")

    def weights(t, g):
        i = work[BLOCK_AT + t]
        p = work[PAIR_AT + t]
        a = work[i * LIST + 2 * p]
        b = work[i * LIST + 2 * p + 1]
        slot = i // 4 * 4 + lax.rem(my_x - i % 4 + 4, 4)
        cols = slice(g * 256, (g + 1) * 256)
        keys = jnp.concatenate([kvs[a, :, cols], kvs[b, :, cols]], axis=0)
        queries = q_all[slot, :, cols]
        spread = jnp.concatenate([jnp.where(head == h, queries, jnp.zeros_like(queries)) for h in range(4)], axis=0)
        score = lax.dot_general(spread, keys, LAST_DIMS, preferred_element_type=jnp.float32)
        return (score + score * jnp.tanh(score)).astype(jnp.bfloat16)

    def attended(t, g, weight):
        i = work[BLOCK_AT + t]
        p = work[PAIR_AT + t]
        a = work[i * LIST + 2 * p]
        b = work[i * LIST + 2 * p + 1]
        cols = slice(D + g * 256, D + (g + 1) * 256)
        values = jnp.concatenate([kvs[a, :, cols], kvs[b, :, cols]], axis=0)
        every = jnp.dot(weight, values, preferred_element_type=jnp.float32)
        mine = every[:BLK]
        for h in range(1, 4):
            mine = jnp.where(head == h, every[h * BLK : (h + 1) * BLK], mine)
        return mine

    def fill(n, slot):
        for u in range(AT_ONCE):
            for g in range(2):
                held[slot, u, g] = weights(n * AT_ONCE + u, g)

    arrived = ensure(0, jnp.int32(0))
    fill(0, 0)

    def step(n, arrived):
        now = n % 2
        arrived = ensure(n + 1, arrived)
        sums = [attended(n * AT_ONCE + u, g, held[now, u, g]) for u in range(AT_ONCE) for g in range(2)]
        fill(n + 1, 1 - now)
        for u in range(AT_ONCE):
            i = work[BLOCK_AT + n * AT_ONCE + u]
            for g in range(2):
                acc[i, :, g * 256 : (g + 1) * 256] += sums[2 * u + g]
        return arrived

    arrived = lax.fori_loop(0, (total + AT_ONCE - 1) // AT_ONCE, step, arrived)
    lax.fori_loop(arrived, count, arrive, 0)
    for i in range(8):
        for z in range(2):
            for y in range(4):
                first = z * 64 + y * 16
                out_ref[i % 4 * 4 + y, i // 4 * 2 + z] = acc[i, first : first + 16, :].astype(jnp.bfloat16)


def attend(work, queries, own, oth):
    smem = pl.BlockSpec(memory_space=pltpu.SMEM)
    vmem = pl.BlockSpec(memory_space=pltpu.VMEM)
    hbm = pl.BlockSpec(memory_space=pltpu.HBM)
    return pl.pallas_call(
        attend_kernel,
        in_specs=[smem] + [vmem] * 8 + [hbm] * 2,
        out_specs=vmem,
        scratch_shapes=[
            pltpu.VMEM((OWN + 1, BLK, 2 * D), jnp.bfloat16),
            pltpu.VMEM((8, BLK, D), jnp.bfloat16),
            pltpu.VMEM((8, BLK, D), jnp.float32),
            pltpu.VMEM((2, AT_ONCE, 2, 4 * BLK, 256), jnp.bfloat16),
            pltpu.SemaphoreType.DMA((OWN,)),
        ],
        out_shape=jax.ShapeDtypeStruct((16, 4, 16, D), jnp.bfloat16),
        compiler_params=pltpu.CompilerParams(vmem_limit_bytes=ATTEND_VMEM),
        cost_estimate=pl.CostEstimate(flops=20_000_000_000, bytes_accessed=8_000_000, transcendentals=0),
        name="attend",
    )(work, *queries, own, oth)


def place_sums_kernel(parts_ref, out_ref):
    core, zh = lax.axis_index("c"), lax.axis_index("zh")
    sums = jnp.sum(parts_ref[...].astype(jnp.float32), axis=0)
    near, far = sums[:32], sums[32:]
    halves = [jnp.where(zh == 0, near, far), jnp.where(zh == 0, far, near)]
    for z in range(2):
        for parity in range(2):
            mine = jnp.where(core == parity, halves[z], 0.0).astype(jnp.bfloat16)
            for k in range(4):
                out_ref[z * 8 + parity * 4 + k] = mine[k * 8 : (k + 1) * 8]


def place_sums(parts):
    vmem = pl.BlockSpec(memory_space=pltpu.VMEM)
    return pl.pallas_call(
        place_sums_kernel,
        in_specs=[vmem],
        out_specs=vmem,
        out_shape=jax.ShapeDtypeStruct((16, 8, D), jnp.bfloat16),
        compiler_params=pltpu.CompilerParams(vmem_limit_bytes=16 * 1024 * 1024),
        name="place_sums",
    )(parts)


def on_device(candidates, norm_gain, qu_weight, out_weight, kv_cache, requests, block_mask, hist_len):
    oth_cache = shift(kv_cache, "c", 1)

    wanted = requests[0]
    asker = jnp.bitwise_xor(jnp.arange(32)[:, None, None, None], jnp.arange(128)[None, None, :, None])
    to_holder = jnp.sum(jnp.where(((wanted >> 5) & 31) == asker, (wanted & (OWN - 1)) + 1, 0), axis=3)
    asked = lax.all_to_all(to_holder, HIST, 0, 0, tiled=True)

    rows = lax.dynamic_slice_in_dim(candidates, lax.axis_index("c") * BLK, BLK, 0)
    across = shift(rows, "zh", 1)
    zh, x, zl, y = (lax.axis_index(a) for a in AXES[:4])
    first_slot = (((zh * 4 + x) * 4 + zl) * 4 + y) * SLOTS
    mask = lax.dynamic_slice_in_dim(block_mask, first_slot, SLOTS, 1)
    lens = lax.dynamic_slice_in_dim(hist_len, first_slot, SLOTS, 0)
    across, asked, mask, lens = lax.optimization_barrier((across, asked, mask, lens))
    near, far = project(rows, across, norm_gain, qu_weight)
    near_1, far_1, near_3, far_3 = shift(near, "x", 1), shift(far, "x", 1), shift(near, "x", -1), shift(far, "x", -1)
    near_2, far_2 = shift(near_1, "x", 1), shift(far_3, "x", -1)
    queries = (near, near_1, near_2, near_3, far, far_1, far_2, far_3)

    sums = attend(plan(asked, mask, lens), queries, kv_cache, oth_cache)

    parts = lax.all_to_all(sums.reshape(16, 64, D), ("x", "y"), 0, 0, tiled=True)
    parts = lax.all_to_all(place_sums(parts), ("zh", "zl", "c"), 0, 0, tiled=True)
    gate = project_gate(candidates, norm_gain, qu_weight)
    return finish(parts, gate, candidates, out_weight)


def solution(mesh):
    fine = Mesh(mesh.devices.reshape(2, 4, 4, 4, 2), AXES)
    placed = (
        P(CAND, None),
        P(),
        P(),
        P(),
        P(AXES, None, None),
        P(AXES, None),
        P(),
        P(),
    )
    return jax.shard_map(on_device, mesh=fine, in_specs=placed, out_specs=P(AXES, None), check_vma=False)
```

```python
import functools

import jax
import jax.numpy as jnp
from jax import lax
from jax.experimental import pallas as pl
from jax.experimental.pallas import tpu as pltpu
from jax.sharding import Mesh, PartitionSpec as P

H = 8
DH = 64
D = H * DH
BLK = 128
OWN = 32
EPS = 1e-05
HALF_SCALE = 0.0625
LAST_DIMS = (((1,), (1,)), ((), ()))
AXES = ("zh", "x", "zl", "y", "c")
CAND = ("zh", "x")
HIST = ("zl", "y", "c")
SLOTS = 2 * OWN
AT_ONCE = 4
ITEMS = 4 * OWN + 4 * AT_ONCE
LIST = OWN + 4
BLOCK_AT = 8 * LIST
PAIR_AT = BLOCK_AT + ITEMS
SOURCE_AT = PAIR_AT + ITEMS
ROWS_AT = SOURCE_AT + OWN + 8
TOTAL_AT = ROWS_AT + OWN + 8
PLAN = TOTAL_AT + 8


PROJECT_VMEM = 54016 * 1024
ATTEND_VMEM = 53760 * 1024


def normalize_input(values, norm_gain):
    center = jnp.mean(values, axis=-1, keepdims=True)
    spread = jnp.mean(jnp.square(values - center), axis=-1, keepdims=True)
    return ((values - center) * lax.rsqrt(spread + EPS) * norm_gain).astype(jnp.bfloat16)


def silu(values):
    half = 0.5 * values
    return half + half * jnp.tanh(half)


def shift(value, axis, steps):
    count = lax.axis_size(axis)
    return lax.ppermute(value, axis, [(i, (i + steps) % count) for i in range(count)])


def project_kernel(near_rows, far_rows, gain, weight_hbm, near_ref, far_ref, weight, sem):
    copy = pltpu.make_async_copy(weight_hbm.at[:, pl.ds(0, D)], weight, sem)
    copy.start()
    rows = jnp.concatenate([near_rows[...], far_rows[...]], axis=0).astype(jnp.float32)
    normed = normalize_input(rows, gain[:1])
    copy.wait()
    projected = jnp.dot(normed, weight[...], preferred_element_type=jnp.float32)
    queries = silu(projected).astype(jnp.bfloat16) * jnp.bfloat16(HALF_SCALE)
    near_ref[...] = queries[:BLK]
    far_ref[...] = queries[BLK:]


def project(near, far, gain, qu_weight):
    vmem = pl.BlockSpec(memory_space=pltpu.VMEM)
    hbm = pl.BlockSpec(memory_space=pltpu.HBM)
    return pl.pallas_call(
        project_kernel,
        in_specs=[vmem] * 3 + [hbm],
        out_specs=[vmem] * 2,
        scratch_shapes=[
            pltpu.VMEM((D, D), jnp.bfloat16),
            pltpu.SemaphoreType.DMA,
        ],
        out_shape=[jax.ShapeDtypeStruct((BLK, D), jnp.bfloat16)] * 2,
        compiler_params=pltpu.CompilerParams(vmem_limit_bytes=PROJECT_VMEM),
        name="project",
    )(near, far, gain, qu_weight)


def output_rows():
    return pl.ds(pl.multiple_of((lax.axis_index("zl") * 4 + lax.axis_index("y")) * 16, 16), 16)


def gate_kernel(cand_ref, gain_ref, weight_ref, gate_ref):
    rows = cand_ref[output_rows(), :].astype(jnp.float32)
    normed = normalize_input(rows, gain_ref[...])
    gate_ref[...] = silu(jnp.dot(normed, weight_ref[:, D:], preferred_element_type=jnp.float32))


def project_gate(candidates, norm_gain, qu_weight):
    vmem = pl.BlockSpec(memory_space=pltpu.VMEM)
    return pl.pallas_call(
        gate_kernel,
        in_specs=[vmem] * 3,
        out_specs=vmem,
        out_shape=jax.ShapeDtypeStruct((16, D), jnp.float32),
        compiler_params=pltpu.CompilerParams(vmem_limit_bytes=16 * 1024 * 1024),
        name="gate",
    )(candidates, norm_gain.reshape(1, D), qu_weight)


def finish_kernel(parts_ref, gate_ref, cand_ref, weight_ref, out_ref):
    summed = jnp.sum(parts_ref[...].astype(jnp.float32), axis=0)
    core = lax.axis_index("c")
    gate = jnp.where(core == 0, gate_ref[:8], gate_ref[8:])
    rows = cand_ref[output_rows(), :].astype(jnp.float32)
    rows = jnp.where(core == 0, rows[:8], rows[8:])
    heads = []
    for h in range(H):
        one = summed[:, h * DH : (h + 1) * DH]
        center = jnp.mean(one, axis=-1, keepdims=True)
        spread = jnp.mean(jnp.square(one - center), axis=-1, keepdims=True)
        heads.append((one - center) * lax.rsqrt(spread + EPS))
    mixed = (jnp.concatenate(heads, axis=1) * gate).astype(jnp.bfloat16)
    output = rows + jnp.dot(mixed, weight_ref[...], preferred_element_type=jnp.float32)
    out_ref[...] = output.astype(jnp.bfloat16)


def finish(parts, gate, candidates, out_weight):
    vmem = pl.BlockSpec(memory_space=pltpu.VMEM)
    return pl.pallas_call(
        finish_kernel,
        in_specs=[vmem] * 4,
        out_specs=vmem,
        out_shape=jax.ShapeDtypeStruct((8, D), jnp.bfloat16),
        compiler_params=pltpu.CompilerParams(vmem_limit_bytes=16 * 1024 * 1024),
        name="finish",
    )(parts, gate, candidates, out_weight)


def mark_used(asked, work, used):
    for s in range(SLOTS + 1):
        used[s] = 0
    for k in range(32):
        for other in range(2):
            value = asked[k, 0, other]
            used[jnp.where(value > 0, 2 * value - 2 + other, SLOTS)] = 1
    place = jnp.int32(0)
    for s in range(SLOTS):
        work[SOURCE_AT + place] = s
        place = place + used[s]
    return place


def list_items(mask, lens, count, work):
    core, zh = lax.axis_index("c"), lax.axis_index("zh")
    columns = [core * OWN, (1 - core) * OWN]
    rows = [(jnp.bitwise_xor(zh, i // 4) * 4 + i % 4) * 2 + core for i in range(8)]

    def block(n, counts):
        s = work[SOURCE_AT + n]
        column = jnp.where((s & 1) == 0, columns[0], columns[1]) + (s >> 1)
        work[ROWS_AT + n] = lens[column]
        after = []
        for i in range(8):
            work[i * LIST + counts[i]] = n
            after.append(counts[i] + mask[rows[i], column])
        return tuple(after)

    counts = lax.fori_loop(0, count, block, (jnp.int32(0),) * 8)
    for i in range(8):
        work[i * LIST + counts[i]] = OWN
        work[i * LIST + OWN] = OWN
        work[i * LIST + OWN + 1] = OWN

    pairs = [(counts[i] + 1) // 2 for i in range(8)]
    most = functools.reduce(jnp.maximum, pairs)

    def level(p, n):
        for i in range(8):
            work[BLOCK_AT + n] = i
            work[PAIR_AT + n] = p
            n = n + (pairs[i] > p).astype(jnp.int32)
        return n

    total = lax.fori_loop(0, most, level, jnp.int32(0))
    for k in range(3 * AT_ONCE):
        work[BLOCK_AT + total + k] = 7
        work[PAIR_AT + total + k] = OWN // 2
    return total


def plan_kernel(asked, mask, lens, work, used):
    count = mark_used(asked, work, used)
    work[TOTAL_AT] = list_items(mask, lens, count, work)
    work[TOTAL_AT + 1] = count


def plan(asked, mask, lens):
    smem = pl.BlockSpec(memory_space=pltpu.SMEM)
    return pl.pallas_call(
        plan_kernel,
        in_specs=[smem] * 3,
        out_specs=smem,
        scratch_shapes=[pltpu.SMEM((SLOTS + 8,), jnp.int32)],
        out_shape=jax.ShapeDtypeStruct((PLAN,), jnp.int32),
        compiler_params=pltpu.CompilerParams(vmem_limit_bytes=4 * 1024 * 1024),
        name="plan",
    )(asked, mask, lens)


def attend_kernel(work, *rest):
    *q_refs, own_ref, oth_ref, out_ref, kvs, q_all, acc, held, sem = rest
    total, count = work[TOTAL_AT], work[TOTAL_AT + 1]

    def start(k, _):
        s = work[SOURCE_AT + k]

        @pl.when(s % 2 == 0)
        def _():
            pltpu.make_async_copy(own_ref.at[s >> 1], kvs.at[k], sem.at[k]).start()

        @pl.when(s % 2 == 1)
        def _():
            pltpu.make_async_copy(oth_ref.at[s >> 1], kvs.at[k], sem.at[k]).start()

        return 0

    lax.fori_loop(0, count, start, 0)
    kvs[OWN] = jnp.zeros((BLK, 2 * D), jnp.bfloat16)
    acc[...] = jnp.zeros_like(acc)
    for k, ref in enumerate(q_refs):
        q_all[k] = ref[...]

    def arrive(k, _):
        pltpu.make_async_copy(own_ref.at[0], kvs.at[k], sem.at[k]).wait()

        @pl.when(work[ROWS_AT + k] < BLK)
        def _():
            row = lax.broadcasted_iota(jnp.int32, (BLK, D), 0)
            values = kvs[k, :, D:].astype(jnp.float32)
            kvs[k, :, D:] = jnp.where(row < work[ROWS_AT + k], values, 0.0).astype(jnp.bfloat16)

        return 0

    def ensure(n, arrived):
        upto = arrived
        for u in range(AT_ONCE):
            i = work[BLOCK_AT + n * AT_ONCE + u]
            p = work[PAIR_AT + n * AT_ONCE + u]
            for part in range(2):
                block = work[i * LIST + 2 * p + part]
                upto = jnp.maximum(upto, jnp.where(block < OWN, block + 1, 0))
        lax.fori_loop(arrived, upto, arrive, 0)
        return upto

    head = lax.broadcasted_iota(jnp.int32, (BLK, 256), 1) // DH
    my_x = lax.axis_index("x")

    def weights(t, g):
        i = work[BLOCK_AT + t]
        p = work[PAIR_AT + t]
        a = work[i * LIST + 2 * p]
        b = work[i * LIST + 2 * p + 1]
        slot = i // 4 * 4 + lax.rem(my_x - i % 4 + 4, 4)
        cols = slice(g * 256, (g + 1) * 256)
        keys = jnp.concatenate([kvs[a, :, cols], kvs[b, :, cols]], axis=0)
        queries = q_all[slot, :, cols]
        spread = jnp.concatenate([jnp.where(head == h, queries, jnp.zeros_like(queries)) for h in range(4)], axis=0)
        score = lax.dot_general(spread, keys, LAST_DIMS, preferred_element_type=jnp.float32)
        return (score + score * jnp.tanh(score)).astype(jnp.bfloat16)

    def attended(t, g, weight):
        i = work[BLOCK_AT + t]
        p = work[PAIR_AT + t]
        a = work[i * LIST + 2 * p]
        b = work[i * LIST + 2 * p + 1]
        cols = slice(D + g * 256, D + (g + 1) * 256)
        values = jnp.concatenate([kvs[a, :, cols], kvs[b, :, cols]], axis=0)
        every = jnp.dot(weight, values, preferred_element_type=jnp.float32)
        mine = every[:BLK]
        for h in range(1, 4):
            mine = jnp.where(head == h, every[h * BLK : (h + 1) * BLK], mine)
        return mine

    def fill(n, slot):
        for u in range(AT_ONCE):
            for g in range(2):
                held[slot, u, g] = weights(n * AT_ONCE + u, g)

    arrived = ensure(0, jnp.int32(0))
    fill(0, 0)

    def step(n, arrived):
        now = n % 2
        arrived = ensure(n + 1, arrived)
        sums = [attended(n * AT_ONCE + u, g, held[now, u, g]) for u in range(AT_ONCE) for g in range(2)]
        fill(n + 1, 1 - now)
        for u in range(AT_ONCE):
            i = work[BLOCK_AT + n * AT_ONCE + u]
            for g in range(2):
                acc[i, :, g * 256 : (g + 1) * 256] += sums[2 * u + g]
        return arrived

    arrived = lax.fori_loop(0, (total + AT_ONCE - 1) // AT_ONCE, step, arrived)
    lax.fori_loop(arrived, count, arrive, 0)
    for i in range(8):
        for z in range(2):
            for y in range(4):
                first = z * 64 + y * 16
                out_ref[i % 4 * 4 + y, i // 4 * 2 + z] = acc[i, first : first + 16, :].astype(jnp.bfloat16)


def attend(work, queries, own, oth):
    smem = pl.BlockSpec(memory_space=pltpu.SMEM)
    vmem = pl.BlockSpec(memory_space=pltpu.VMEM)
    hbm = pl.BlockSpec(memory_space=pltpu.HBM)
    return pl.pallas_call(
        attend_kernel,
        in_specs=[smem] + [vmem] * 8 + [hbm] * 2,
        out_specs=vmem,
        scratch_shapes=[
            pltpu.VMEM((OWN + 1, BLK, 2 * D), jnp.bfloat16),
            pltpu.VMEM((8, BLK, D), jnp.bfloat16),
            pltpu.VMEM((8, BLK, D), jnp.float32),
            pltpu.VMEM((2, AT_ONCE, 2, 4 * BLK, 256), jnp.bfloat16),
            pltpu.SemaphoreType.DMA((OWN,)),
        ],
        out_shape=jax.ShapeDtypeStruct((16, 4, 16, D), jnp.bfloat16),
        compiler_params=pltpu.CompilerParams(vmem_limit_bytes=ATTEND_VMEM),
        cost_estimate=pl.CostEstimate(flops=20_000_000_000, bytes_accessed=8_000_000, transcendentals=0),
        name="attend",
    )(work, *queries, own, oth)


def place_sums_kernel(parts_ref, out_ref):
    core, zh = lax.axis_index("c"), lax.axis_index("zh")
    sums = jnp.sum(parts_ref[...].astype(jnp.float32), axis=0)
    near, far = sums[:32], sums[32:]
    halves = [jnp.where(zh == 0, near, far), jnp.where(zh == 0, far, near)]
    for z in range(2):
        for parity in range(2):
            mine = jnp.where(core == parity, halves[z], 0.0).astype(jnp.bfloat16)
            for k in range(4):
                out_ref[z * 8 + parity * 4 + k] = mine[k * 8 : (k + 1) * 8]


def place_sums(parts):
    vmem = pl.BlockSpec(memory_space=pltpu.VMEM)
    return pl.pallas_call(
        place_sums_kernel,
        in_specs=[vmem],
        out_specs=vmem,
        out_shape=jax.ShapeDtypeStruct((16, 8, D), jnp.bfloat16),
        compiler_params=pltpu.CompilerParams(vmem_limit_bytes=16 * 1024 * 1024),
        name="place_sums",
    )(parts)


def on_device(candidates, norm_gain, qu_weight, out_weight, kv_cache, requests, block_mask, hist_len):
    oth_cache = shift(kv_cache, "c", 1)

    wanted = requests[0]
    asker = jnp.bitwise_xor(jnp.arange(32)[:, None, None, None], jnp.arange(128)[None, None, :, None])
    to_holder = jnp.sum(jnp.where(((wanted >> 5) & 31) == asker, (wanted & (OWN - 1)) + 1, 0), axis=3)
    asked = lax.all_to_all(to_holder, HIST, 0, 0, tiled=True)

    rows = lax.dynamic_slice_in_dim(candidates, lax.axis_index("c") * BLK, BLK, 0)
    across = shift(rows, "zh", 1)
    zh, x, zl, y = (lax.axis_index(a) for a in AXES[:4])
    first_slot = (((zh * 4 + x) * 4 + zl) * 4 + y) * SLOTS
    mask = lax.dynamic_slice_in_dim(block_mask, first_slot, SLOTS, 1)
    lens = lax.dynamic_slice_in_dim(hist_len, first_slot, SLOTS, 0)
    gain = jnp.broadcast_to(norm_gain, (8, D))
    across, asked, mask, lens, gain = lax.optimization_barrier((across, asked, mask, lens, gain))
    near, far = project(rows, across, gain, qu_weight)
    near_1, far_1, near_3, far_3 = shift(near, "x", 1), shift(far, "x", 1), shift(near, "x", -1), shift(far, "x", -1)
    near_2, far_2 = shift(near_1, "x", 1), shift(far_3, "x", -1)
    queries = (near, near_1, near_2, near_3, far, far_1, far_2, far_3)

    sums = attend(plan(asked, mask, lens), queries, kv_cache, oth_cache)

    parts = lax.all_to_all(sums.reshape(16, 64, D), ("x", "y"), 0, 0, tiled=True)
    parts = lax.all_to_all(place_sums(parts), ("zh", "zl", "c"), 0, 0, tiled=True)
    gate = project_gate(candidates, norm_gain, qu_weight)
    return finish(parts, gate, candidates, out_weight)


def solution(mesh):
    fine = Mesh(mesh.devices.reshape(2, 4, 4, 4, 2), AXES)
    placed = (
        P(CAND, None),
        P(),
        P(),
        P(),
        P(AXES, None, None),
        P(AXES, None),
        P(),
        P(),
    )
    return jax.shard_map(on_device, mesh=fine, in_specs=placed, out_specs=P(AXES, None), check_vma=False)
```
